256 devices in a mesh: section: 16 (over x_lo, y, core), dp: 16 (over z, x_hi).
Axes of the slice: x: 4 (x_hi: 2, x_lo: 2; x = x_hi * 2 + x_lo), y: 4, z: 8, core: 2. Of those that a mesh axis runs over, the one named last changes fastest.
Arguments:
- x_in: bfloat16 [64, 32, 8192], P('dp'), may hold values from -10 to 10
- segment_ids: int32 [64, 32], P('dp'), may hold values from 0 to 2, never falling along the last dimension, each value on 1 to 16 neighbouring positions
- norm_gain: bfloat16 [16, 8192], P('section'), may hold values from 0.5 to 1.5
- w_attn: bfloat16 [16, 8192, 512], P('section'), may hold values from -2 to 2
- final_gain: bfloat16 [8192], replicated, may hold values from 0.5 to 1.5
- upstream: bfloat16 [64, 32, 8192], P('dp'), may hold values from -6 to 6
Outputs:
- grad_attn: bfloat16 [16, 8192, 512], P('section', 'dp')
The draws below stay inside these ranges and needn't reach their ends.
Inputs may be any that keep to these rules, and one draw needn't show every extreme that they name: `segment_ids`: segment numbers never fall along a row.
All inputs are finite; a program needn't handle non-finite values.
Results may differ from the reference program's by a relative error of at most 0.025.
Values may be sent and summed in bfloat16 or wider, within the bound.
No kernel may reach another device: no remote copies, remote signals or barrier semaphores. Data moves between devices by JAX's collectives and lax.ppermute only.
A program may use at most 128 MiB of HBM per device.

```python
import math
import jax
import jax.numpy as jnp
import numpy as np
from jax import lax

D = 8192
HEAD_DIMENSION = 128
TOK = 32
MB = 4
LAYERS = 16
BATCH = 64
N_DP = 16


def drawn_features(key):
    order = jax.random.permutation(jax.random.fold_in(key, 101), D)
    return (order < D // 4).astype(jnp.float32)


def draw_x_in(key, part):
    marked = drawn_features(key)
    key = jax.random.fold_in(key, 1)
    noise_key, level_key = jax.random.split(key)
    shape = (BATCH, TOK, D)
    choose = jax.random.randint(level_key, (BATCH, TOK), 0, 5)
    levels = jnp.array([0.0, 0.0, 0.5, 0.75, 1.0], jnp.float32)
    noise = jnp.clip(jax.random.normal(noise_key, shape, jnp.float32), -5.0, 5.0)
    strength = levels[choose][..., None]
    return (noise + 4.0 * strength * marked[None, None, :]).astype(jnp.bfloat16)


def draw_w_attn(key, part):
    marked = drawn_features(key)
    key = jax.random.fold_in(key, 2)
    shape = (LAYERS, D, 4 * HEAD_DIMENSION)
    noise = jnp.clip(jax.random.normal(key, shape, jnp.float32), -5.0, 5.0)
    column = jnp.arange(4 * HEAD_DIMENSION)
    inner = column % (HEAD_DIMENSION // 2)
    aligned = ((column < 2 * HEAD_DIMENSION) & (inner >= 3 * HEAD_DIMENSION // 8)).astype(jnp.float32)
    offset = 40.0 * HEAD_DIMENSION ** (-0.25) / D
    planted = offset * marked[:, None] * aligned[None, :]
    return (noise * D ** (-0.5) + planted[None, :, :]).astype(jnp.bfloat16)


def block_scale(rng, shape, cuts, least, top_value):
    def one(axis_at, blocks):
        draws = jax.random.uniform(jax.random.fold_in(jax.random.fold_in(rng, 6), axis_at), (blocks,), jnp.float32, least / len(cuts), top_value / len(cuts))
        return jnp.repeat(jnp.exp(draws), shape[axis_at] // blocks).reshape((-1,) + (1,) * (len(shape) - axis_at - 1))

    level = one(*cuts[0])
    for cut in cuts[1:]:
        level = level * one(*cut)
    return level


def split_up(amount, total, limit, slope):
    weights = [(1 << 20) // math.isqrt(rank ** slope) + 1 for rank in range(2, amount + 1)]
    surplus, given = total - limit - (amount - 1), [1] * (amount - 1)
    while surplus > 0:
        candidates = [i for i in range(amount - 1) if given[i] < limit]
        whole, budget = sum([weights[i] for i in candidates]), surplus
        for i in candidates:
            more = min(limit - given[i], max(1, budget * weights[i] // whole), surplus)
            given[i] = given[i] + more
            surplus = surplus - more
    return np.array([limit] + given)


def ragged(stream_key, amount, total, bound, skew):
    if amount == 2:
        one = jax.random.randint(stream_key, (), max(1, total - bound), min(bound, total - 1) + 1)
        return jnp.stack([one, total - one])
    tallies = jnp.asarray(split_up(amount, total, bound, skew), jnp.int32)
    twos = (amount - 1) // 2
    donor, sink = tallies[1:1 + 2 * twos:2], tallies[2:2 + 2 * twos:2]
    slack = jnp.minimum(donor - 1, bound - sink)
    passed = jax.random.randint(jax.random.fold_in(stream_key, 1), (twos,), 0, 1 << 20) % (slack + 1)
    tallies = tallies.at[1:1 + 2 * twos:2].set(donor - passed).at[2:2 + 2 * twos:2].set(sink + passed)
    return tallies[jax.random.permutation(jax.random.fold_in(stream_key, 2), amount)]


def normal_values(key, dims, width, most, cuts=(), kind=jnp.bfloat16):
    loudness = block_scale(key, dims, cuts, -0.22, 0.18) if cuts else 1.0
    result = jax.random.normal(key, dims, jnp.float32) * width * loudness
    return jnp.minimum(jnp.maximum(result, -most), most).astype(kind)


def setup_inputs(seed: int = 0) -> dict:
    keys = jax.random.split(jax.random.key(seed), 7)
    return {
        "x_in": draw_x_in(jax.random.fold_in(keys[6], 71), 0),
        "segment_ids": jax.vmap(lambda own: jnp.searchsorted(jnp.cumsum(ragged(own, 3, TOK, TOK // 2, 0)), jnp.arange(TOK), side="right"))(jax.random.split(keys[1], BATCH)).reshape((BATCH, TOK)).astype(jnp.int32),
        "norm_gain": jnp.clip(1.0 + 0.1 * jax.random.normal(keys[2], (LAYERS, D), jnp.float32), 0.5, 1.5).astype(jnp.bfloat16),
        "w_attn": draw_w_attn(jax.random.fold_in(keys[6], 71), 0),
        "final_gain": jnp.clip(1.0 + 0.1 * jax.random.normal(keys[4], (D,), jnp.float32), 0.5, 1.5).astype(jnp.bfloat16),
        "upstream": normal_values(keys[5], (BATCH, TOK, D), 1.0, 6.0, ((0, 16),)),
    }


EPSILON = 1e-05
ROTARY_BASE = 500000.0

def normed(value_rows, gain):
    scale = lax.rsqrt(lax.optimization_barrier(jnp.mean(value_rows * value_rows, axis=-1, keepdims=True)) + EPSILON)
    return value_rows * scale * gain.astype(jnp.float32)

def tables(segs):
    index = jnp.arange(TOK, dtype=jnp.int32)
    earlier = lax.optimization_barrier(jnp.sum((segs[:, None, :] < segs[:, :, None]).astype(jnp.int32), axis=-1))
    where_at = (index[None, :] - earlier).astype(jnp.float32)
    half = HEAD_DIMENSION // 2
    freq = ROTARY_BASE ** (-2.0 * jnp.arange(half, dtype=jnp.float32) / HEAD_DIMENSION)
    angle = where_at[..., None] * freq
    cosine = jnp.concatenate([jnp.cos(angle), jnp.cos(angle)], axis=-1)
    sine = jnp.concatenate([jnp.sin(angle), jnp.sin(angle)], axis=-1)
    allowed = (segs[:, :, None] == segs[:, None, :]) & (index[None, :, None] >= index[None, None, :])
    return (cosine, sine, allowed)

def rotate(value_rows, cosine, sine):
    half = value_rows.shape[-1] // 2
    turned = jnp.concatenate([-value_rows[..., half:], value_rows[..., :half]], axis=-1)
    return value_rows * cosine + turned * sine

def attention(qkv, cosine, sine, allowed):
    query_rows = rotate(qkv[..., :HEAD_DIMENSION], cosine, sine)
    key_rows = rotate(qkv[..., HEAD_DIMENSION:2 * HEAD_DIMENSION], cosine, sine)
    value_rows = qkv[..., 2 * HEAD_DIMENSION:]
    attention_scores = jnp.einsum('syt,sht->syh', query_rows, key_rows, precision=lax.Precision.HIGHEST) * HEAD_DIMENSION ** (-0.5)
    attention_scores = jnp.where(allowed, attention_scores, -1e+30)
    attention_probabilities = jax.nn.softmax(attention_scores, axis=-1)
    return jnp.einsum('wom,wmz->woz', attention_probabilities, value_rows, precision=lax.Precision.HIGHEST)

def layer_forward(hidden_states, gain, weights, cosine, sine, allowed):
    flat = hidden_states.astype(jnp.float32).reshape(-1, D)
    xnorm = normed(flat, gain).astype(jnp.bfloat16)
    qkv = jnp.dot(xnorm, weights[:, :3 * HEAD_DIMENSION], preferred_element_type=jnp.float32).reshape(hidden_states.shape[0], TOK, 3 * HEAD_DIMENSION)
    heads = attention(qkv, cosine, sine, allowed).astype(jnp.bfloat16).reshape(-1, HEAD_DIMENSION)
    branch = lax.dot_general(heads, weights[:, 3 * HEAD_DIMENSION:], (((1,), (1,)), ((), ())), preferred_element_type=jnp.float32)
    return (flat + branch).astype(jnp.bfloat16).reshape(hidden_states.shape)

def layer_backward(hidden_states, grad_out, gain, weights, cosine, sine, allowed):
    flat = hidden_states.astype(jnp.float32).reshape(-1, D)
    xnorm = normed(flat, gain).astype(jnp.bfloat16)
    qkv = jnp.dot(xnorm, weights[:, :3 * HEAD_DIMENSION], preferred_element_type=jnp.float32).reshape(hidden_states.shape[0], TOK, 3 * HEAD_DIMENSION)
    heads32, pull = jax.vjp(lambda a: attention(a, cosine, sine, allowed), qkv)
    heads = heads32.astype(jnp.bfloat16).reshape(-1, HEAD_DIMENSION)
    grad_flat = grad_out.reshape(-1, D)
    grad_heads = jnp.dot(grad_flat, weights[:, 3 * HEAD_DIMENSION:], preferred_element_type=jnp.float32).reshape(heads32.shape)
    grad_qkv = pull(grad_heads)[0].astype(jnp.bfloat16).reshape(-1, 3 * HEAD_DIMENSION)
    grad_norm = lax.dot_general(grad_qkv, weights[:, :3 * HEAD_DIMENSION], (((1,), (1,)), ((), ())), preferred_element_type=jnp.float32)
    _, norm_pull = jax.vjp(lambda a: normed(a, gain), flat)
    grad_in = (grad_flat.astype(jnp.float32) + norm_pull(grad_norm)[0]).astype(jnp.bfloat16).reshape(hidden_states.shape)
    left = lax.dot_general(xnorm, grad_qkv, (((0,), (0,)), ((), ())), preferred_element_type=jnp.float32)
    right = lax.dot_general(grad_flat, heads, (((0,), (0,)), ((), ())), preferred_element_type=jnp.float32)
    return (grad_in, jnp.concatenate([left, right], axis=1))

def head_backward(hidden_states, final_gain, upstream):
    flat = hidden_states.astype(jnp.float32).reshape(-1, D)
    _, pull = jax.vjp(lambda a: normed(a, final_gain), flat)
    return pull(upstream.astype(jnp.float32).reshape(-1, D))[0].astype(jnp.bfloat16).reshape(hidden_states.shape)

def reference(x_in, segment_ids, norm_gain, w_attn, final_gain, upstream):

    def replica(total, which):
        first = (which * MB).astype(jnp.int32)
        hidden_states = lax.dynamic_slice_in_dim(x_in, first, MB, 0)
        segs = lax.dynamic_slice_in_dim(segment_ids, first, MB, 0)
        cotangent = lax.dynamic_slice_in_dim(upstream, first, MB, 0)
        cosine, sine, allowed = tables(segs)
        stash = []
        for layer in range(LAYERS):
            stash.append(hidden_states)
            hidden_states = layer_forward(hidden_states, norm_gain[layer], w_attn[layer], cosine, sine, allowed)
        grad = head_backward(hidden_states, final_gain, cotangent)
        terms = [None] * LAYERS
        for layer in range(LAYERS - 1, -1, -1):
            grad, terms[layer] = layer_backward(stash[layer], grad, norm_gain[layer], w_attn[layer], cosine, sine, allowed)
        rounded = lax.optimization_barrier(jnp.stack(terms).astype(jnp.bfloat16))
        return (total + rounded.astype(jnp.float32), None)
    total = jnp.zeros((LAYERS, D, 4 * HEAD_DIMENSION), jnp.float32)
    total, _ = lax.scan(replica, total, jnp.arange(N_DP, dtype=jnp.int32))
    return total.astype(jnp.bfloat16)
```

```python
import functools

import jax
import jax.numpy as jnp
from jax import lax
from jax.experimental import pallas as pl
from jax.experimental.pallas import tpu as pltpu
from jax.sharding import PartitionSpec as P

EPSILON = 1e-05
ROTARY_BASE = 500000.0
F32 = jnp.float32
BF16 = jnp.bfloat16
NN = (((1,), (0,)), ((), ()))
NT = (((1,), (1,)), ((), ()))
TN = (((0,), (0,)), ((), ()))


def mm(a, b, dims=NN):
    return lax.dot_general(a, b, dims, preferred_element_type=F32)


def split(a):
    high = a.astype(BF16)
    return high, (a - high.astype(F32)).astype(BF16)


def mm3(a, b, dims=NN):
    (ah, al), (bh, bl) = a, b
    return mm(ah, bh, dims) + (mm(al, bh, dims) + mm(ah, bl, dims))


def rowsum(a):
    return jnp.sum(a, axis=1, keepdims=True)


def scan_kernel(
    layers, width, hd,
    blocks, base, stats, cosine, sine, allowed,
    zo, final_scale,
    cols, diag, outs, grads, q_keep, k_keep, v_keep, p_keep, r_keep, s_keep, col_sem, diag_sem,
):
    first = [l * (l - 1) // 2 for l in range(layers + 1)]

    def copies(l):
        span = pl.ds(first[l], l)
        return (
            pltpu.make_async_copy(
                blocks.at[l, pl.ds(0, l)], cols.at[span, :, pl.ds(0, 2 * hd)], col_sem.at[0, l]
            ),
            pltpu.make_async_copy(
                blocks.at[pl.ds(0, l), l], cols.at[span, :, pl.ds(2 * hd, 2 * hd)], col_sem.at[1, l]
            ),
        )

    def diag_copy(l):
        return pltpu.make_async_copy(blocks.at[l, l, :, pl.ds(0, hd)], diag.at[l], diag_sem.at[l])

    diag_copy(0).start()
    for l in range(1, layers):
        for c in copies(l):
            c.start()
        diag_copy(l).start()

    def rope(u):
        return u * cosine[...] + pltpu.roll(u, hd // 2, 1) * sine[...]

    def rope_back(w):
        return w * cosine[...] - pltpu.roll(w, hd // 2, 1) * sine[...]

    scale = hd ** (-0.5)
    inv_width = 1.0 / width
    square = stats[:, 0:1]
    reach = stats[:, 1:2]
    for l in range(layers):
        if l:
            for c in copies(l):
                c.wait()
        diag_copy(l).wait()
        own = base[l]
        acc = jnp.concatenate(
            [
                own[:, : 2 * hd].astype(F32) + own[:, 2 * hd : 4 * hd].astype(F32),
                own[:, 4 * hd : 6 * hd].astype(F32),
            ],
            axis=1,
        )
        if l:
            rows = cols[pl.ds(first[l], l)].reshape(l * hd, 4 * hd)
            acc = acc + mm(outs[:, pl.ds(0, l * hd)], rows)
        s = lax.rsqrt(square * inv_width + EPSILON)
        q = rope(acc[:, :hd] * s)
        k = rope(acc[:, hd : 2 * hd] * s)
        v = acc[:, 2 * hd : 3 * hd] * s
        reached = acc[:, 3 * hd :]
        scores = mm3(split(q), split(k), NT) * scale
        scores = jnp.where(allowed[...] > 0.0, scores, -1e30)
        e = jnp.exp(scores - jnp.max(scores, axis=1, keepdims=True))
        p = e / rowsum(e)
        o = mm(p.astype(BF16), v.astype(BF16)).astype(BF16)
        outs[:, pl.ds(l * hd, hd)] = o
        zo[l, :, pl.ds(4 * hd, hd)] = o
        o32 = o.astype(F32)
        turned = mm(o, diag[l])
        square = square + rowsum(o32 * (2.0 * reached + turned))
        reach = reach + rowsum(o32 * own[:, 6 * hd :].astype(F32))
        q_keep[l] = q
        k_keep[l] = k
        v_keep[l] = v
        p_keep[l] = p
        r_keep[l] = reached + turned
        s_keep[l] = jnp.broadcast_to(s, (s.shape[0], hd))

    s_last = lax.rsqrt(square * inv_width + EPSILON)
    final_scale[...] = jnp.broadcast_to(s_last, final_scale.shape)
    back = s_last * s_last * s_last * inv_width * reach
    for l in range(layers):
        grads[:, pl.ds(l * hd, hd)] = s_last * base[l, :, pl.ds(6 * hd, hd)].astype(F32)

    for l in range(layers - 1, -1, -1):
        d_o = grads[:, pl.ds(l * hd, hd)] - back * r_keep[l]
        p, q, k, v, s = p_keep[l], q_keep[l], k_keep[l], v_keep[l], s_keep[l]
        d_o16 = d_o.astype(BF16)
        d_v = mm(p.astype(BF16), d_o16, TN)
        d_p = mm(d_o16, v.astype(BF16), NT)
        d_s = p * (d_p - rowsum(d_p * p)) * scale
        ds = split(d_s)
        d_q = mm3(ds, split(k))
        d_k = mm3(ds, split(q), TN)
        c = rowsum(d_q * q + d_k * k + d_v * v) * (s[:, 0:1] * s[:, 0:1]) * inv_width
        o32 = outs[:, pl.ds(l * hd, hd)].astype(F32)
        z = jnp.concatenate(
            [rope_back(d_q) * s, rope_back(d_k) * s, d_v * s, -(back * o32)], axis=1
        ).astype(BF16)
        zo[l, :, pl.ds(0, 4 * hd)] = z
        if l:
            rows = cols[pl.ds(first[l], l)].reshape(l * hd, 4 * hd)
            grads[:, pl.ds(0, l * hd)] += mm(z, rows, NT)
        back = back + c


def scan_layers(blocks, base, stats, cosine, sine, allowed, width):
    layers, _, hd, _ = blocks.shape
    rows = base.shape[1]
    vmem = pl.BlockSpec(memory_space=pltpu.VMEM)
    keep = pltpu.VMEM((layers, rows, hd), F32)
    return pl.pallas_call(
        functools.partial(scan_kernel, layers, width, hd),
        out_shape=(
            jax.ShapeDtypeStruct((layers, rows, 5 * hd), BF16),
            jax.ShapeDtypeStruct((rows, hd), F32),
        ),
        in_specs=[pl.BlockSpec(memory_space=pl.ANY)] + [vmem] * 5,
        out_specs=(vmem, vmem),
        scratch_shapes=[
            pltpu.VMEM((layers * (layers - 1) // 2, hd, 4 * hd), BF16),
            pltpu.VMEM((layers, hd, hd), BF16),
            pltpu.VMEM((rows, layers * hd), BF16),
            pltpu.VMEM((rows, layers * hd), F32),
            keep, keep, keep, keep, keep, keep,
            pltpu.SemaphoreType.DMA((2, layers)),
            pltpu.SemaphoreType.DMA((layers,)),
        ],
        compiler_params=pltpu.CompilerParams(vmem_limit_bytes=48 * 1024 * 1024),
        cost_estimate=pl.CostEstimate(
            flops=2 * 3 * layers * layers * rows * hd * 4 * hd,
            bytes_accessed=2 * layers * layers * hd * 2 * hd + 4 * layers * rows * 8 * hd,
            transcendentals=layers * rows * rows,
        ),
        name="scan_layers",
    )(blocks, base, stats, cosine, sine, allowed)


def swapped(block):
    n = lax.axis_size("section")
    return lax.ppermute(
        block, ("section", "dp"), [(a * n + b, b * n + a) for a in range(n) for b in range(n)]
    )


def partner(block):
    n = lax.axis_size("section")
    return lax.ppermute(block, "section", [(i, i ^ 1) for i in range(n)])


def all_of_dp(block):
    n = lax.axis_size("dp")
    return lax.all_to_all(jnp.broadcast_to(block[None], (n,) + block.shape), "dp", 0, 0)


def tables(segs, head_size):
    batch, length = segs.shape
    index = jnp.arange(length, dtype=jnp.int32)
    earlier = jnp.sum((segs[:, None, :] < segs[:, :, None]).astype(jnp.int32), axis=-1)
    where_at = (index[None, :] - earlier).astype(F32).reshape(batch * length)
    half = head_size // 2
    freq = ROTARY_BASE ** (-2.0 * jnp.arange(half, dtype=F32) / head_size)
    angle = where_at[:, None] * freq
    cosine, sine = jnp.cos(angle), jnp.sin(angle)
    flat = segs.reshape(batch * length)
    token = jnp.arange(batch * length, dtype=jnp.int32)
    allowed = (
        (flat[:, None] == flat[None, :])
        & (token[:, None] >= token[None, :])
        & (token[:, None] // length == token[None, :] // length)
    )
    return (
        jnp.concatenate([cosine, cosine], axis=-1),
        jnp.concatenate([-sine, sine], axis=-1),
        allowed.astype(F32),
    )


def three(a):
    high = a.astype(BF16)
    rest = a - high.astype(F32)
    middle = rest.astype(BF16)
    return [high, middle, (rest - middle.astype(F32)).astype(BF16)]


def local(x_in, segment_ids, norm_gain, w_attn, final_gain, upstream, scan=scan_layers):
    n = lax.axis_size("section")
    me = lax.axis_index("section")
    row = lax.axis_index("dp")
    micro_count, tok_count, width = x_in.shape
    rows = micro_count * tok_count
    part = width // n
    gain = norm_gain[0].astype(F32)
    weights = w_attn[0]
    hd = weights.shape[1] // 4
    w_in, w_out = weights[:, : 3 * hd], weights[:, 3 * hd :]
    x = x_in.reshape(rows, width)
    up = upstream.reshape(rows, width)
    x32, up32 = x.astype(F32), up.astype(F32)

    half = width // 2
    sent = lax.dynamic_slice_in_dim(w_out, (row % 2) * half, half, 0)
    mine = swapped(sent)
    other = partner(mine)
    odd = me % 2 == 1
    theirs = jnp.concatenate([jnp.where(odd, other, mine), jnp.where(odd, mine, other)], axis=0)

    w_scaled = jnp.concatenate(
        [w_in.astype(F32) * gain[:, None], w_out.astype(F32)], axis=1
    ).astype(BF16)
    tokens = jnp.concatenate(
        [
            lax.dynamic_slice_in_dim(x, me * part, part, 1),
            (lax.dynamic_slice_in_dim(up32, me * part, part, 1)
             * lax.dynamic_slice_in_dim(final_gain.astype(F32), me * part, part, 0)).astype(BF16),
        ],
        axis=0,
    )
    tokens = swapped(tokens)
    slices = lax.all_gather(
        jnp.concatenate([lax.dynamic_slice_in_dim(w_scaled, row * part, part, 0), tokens.reshape(-1, 4 * hd)], axis=0),
        "section",
    )

    up_gain = up32 * final_gain.astype(F32)
    first = mm((x32 * gain).astype(BF16), w_in)
    second = mm(jnp.concatenate([x, up_gain.astype(BF16)], axis=0), w_out)
    high, low = split(first[:, : 2 * hd])
    square = jnp.sum(x32 * x32, axis=1, keepdims=True)
    reach = jnp.sum(x32 * up_gain, axis=1, keepdims=True)
    segs = segment_ids.reshape(rows, 1).astype(BF16)
    extra = jnp.concatenate(
        three(square) + three(reach) + [segs, jnp.zeros((rows, hd - 7), BF16)], axis=1
    )
    packed = swapped(
        jnp.concatenate(
            [high, low, first[:, 2 * hd :].astype(BF16), second[:rows].astype(BF16),
             second[rows:].astype(BF16), extra],
            axis=1,
        )
    )
    base = all_of_dp(packed[:, : 7 * hd])
    extra = packed[:, 7 * hd :].astype(F32)
    stats = jnp.concatenate([rowsum(extra[:, :3]), rowsum(extra[:, 3:6])], axis=1)
    cosine, sine, allowed = tables(
        extra[:, 6].astype(jnp.int32).reshape(micro_count, tok_count), hd
    )

    block = jnp.concatenate(
        [mm((theirs.astype(F32) * gain[:, None]).astype(BF16), w_in, TN), mm(theirs, w_out, TN)],
        axis=1,
    ).astype(BF16)
    returned = swapped(block[:, 2 * hd :])
    on_diag = jnp.concatenate([block[:, 3 * hd :], jnp.zeros((hd, hd), BF16)], axis=1)
    shard = jnp.where(row < me, block[:, : 2 * hd], jnp.where(row == me, on_diag, returned))
    blocks = lax.all_gather(all_of_dp(shard), "section")

    zo, final_scale = scan(blocks, base, stats, cosine, sine, allowed, width)

    s_high, s_low = split(final_scale)
    pair_in = jnp.concatenate(
        [lax.dynamic_index_in_dim(zo, row, 0, keepdims=False),
         jnp.where(lax.broadcasted_iota(jnp.int32, s_high.shape, 1) < hd // 2, s_high, s_low)],
        axis=1,
    )
    pair = lax.all_gather(pair_in, "section").reshape(n * rows, 6 * hd)
    own = lax.all_to_all(zo, "section", 0, 0).reshape(n * rows, 5 * hd)
    z_own, o_own = own[:, : 4 * hd], own[:, 4 * hd :]
    z_pair, o_pair = pair[:, : 4 * hd], pair[:, 4 * hd : 5 * hd]
    below = row < me
    link = mm(jnp.where(below, o_pair, o_own), jnp.where(below, z_own, z_pair), TN).astype(BF16)
    links = all_of_dp(link)

    w_all = slices[:, :part]
    tokens_all = slices[:, part:].reshape(n, 2, rows, part)
    x_all = tokens_all[:, 0].reshape(n * rows, part)
    up_all = tokens_all[:, 1].reshape(n * rows, part)
    s_all = (
        pair[:, 5 * hd : 5 * hd + 1].astype(F32) + pair[:, 5 * hd + hd // 2 : 5 * hd + hd // 2 + 1].astype(F32)
    )
    index = lax.broadcasted_iota(jnp.int32, (n, 1, 1), 0)
    zero = jnp.zeros((), BF16)
    left_links = jnp.where(index < me, links, zero)
    column = lax.broadcasted_iota(jnp.int32, (1, 1, 4 * hd), 2)
    right_links = jnp.where(
        (index > me) | ((index == me) & (column >= 3 * hd)), links, zero
    )
    full = mm(x_all, z_own, TN) + lax.dot_general(
        w_all[:, :, 3 * hd :], left_links, (((0, 2), (0, 1)), ((), ())), preferred_element_type=F32
    )
    right = mm(up_all, (s_all * o_own.astype(F32)).astype(BF16), TN) + lax.dot_general(
        w_all, right_links, (((0, 2), (0, 2)), ((), ())), preferred_element_type=F32
    )
    gain_part = lax.dynamic_slice_in_dim(gain, row * part, part, 0)[:, None]
    return jnp.concatenate(
        [full[:, : 3 * hd] * gain_part, full[:, 3 * hd :] + right], axis=1
    ).astype(BF16)[None]


def solution(mesh):
    placed = (
        P("dp", None, None),
        P("dp", None),
        P("section", None),
        P("section", None, None),
        P(),
        P("dp", None, None),
    )
    return jax.shard_map(
        local, mesh=mesh, in_specs=placed, out_specs=P("section", "dp", None), check_vma=False
    )
```

```python
import functools

import jax
import jax.numpy as jnp
from jax import lax
from jax.experimental import pallas as pl
from jax.experimental.pallas import tpu as pltpu
from jax.sharding import PartitionSpec as P

EPSILON = 1e-05
ROTARY_BASE = 500000.0
F32 = jnp.float32
BF16 = jnp.bfloat16
NN = (((1,), (0,)), ((), ()))
NT = (((1,), (1,)), ((), ()))
TN = (((0,), (0,)), ((), ()))


def mm(a, b, dims=NN):
    return lax.dot_general(a, b, dims, preferred_element_type=F32)


def split(a):
    high = a.astype(BF16)
    return high, (a - high.astype(F32)).astype(BF16)


def mm3(a, b, dims=NN):
    (ah, al), (bh, bl) = a, b
    return mm(ah, bh, dims) + (mm(al, bh, dims) + mm(ah, bl, dims))


def rowsum(a):
    return jnp.sum(a, axis=1, keepdims=True)


def scan_kernel(
    layers, width, hd,
    pick, blocks, base, stats, cosine, sine, allowed,
    zo, factors,
    cols, diag, outs, grads, q_keep, k_keep, v_keep, p_keep, r_keep, s_keep, col_sem, diag_sem,
):
    first = [l * (l - 1) // 2 for l in range(layers + 1)]

    def copies(l):
        span = pl.ds(first[l], l)
        return (
            pltpu.make_async_copy(
                blocks.at[l, pl.ds(0, l)], cols.at[span, :, pl.ds(0, 2 * hd)], col_sem.at[0, l]
            ),
            pltpu.make_async_copy(
                blocks.at[pl.ds(0, l), l], cols.at[span, :, pl.ds(2 * hd, 2 * hd)], col_sem.at[1, l]
            ),
        )

    def diag_copy(l):
        return pltpu.make_async_copy(blocks.at[l, l, :, pl.ds(0, hd)], diag.at[l], diag_sem.at[l])

    diag_copy(0).start()
    for l in range(1, layers):
        for c in copies(l):
            c.start()
        diag_copy(l).start()

    def place(l):
        c = pick[0] ^ l
        return ((pick[1] // 2 + layers // 2 - c // 2) % (layers // 2)) * 2 + ((c ^ pick[1]) & 1)

    def rope(u):
        return u * cosine[...] + pltpu.roll(u, hd // 2, 1) * sine[...]

    def rope_back(w):
        return w * cosine[...] - pltpu.roll(w, hd // 2, 1) * sine[...]

    scale = hd ** (-0.5)
    inv_width = 1.0 / width
    square = stats[:, 0:1]
    reach = stats[:, 1:2]
    for l in range(layers):
        if l:
            for c in copies(l):
                c.wait()
        diag_copy(l).wait()
        own = base[place(l)]
        acc = jnp.concatenate(
            [
                own[:, : 2 * hd].astype(F32) + own[:, 2 * hd : 4 * hd].astype(F32),
                own[:, 4 * hd : 6 * hd].astype(F32),
            ],
            axis=1,
        )
        if l:
            rows = cols[pl.ds(first[l], l)].reshape(l * hd, 4 * hd)
            acc = acc + mm(outs[:, pl.ds(0, l * hd)], rows)
        s = lax.rsqrt(square * inv_width + EPSILON)
        q = rope(acc[:, :hd] * s)
        k = rope(acc[:, hd : 2 * hd] * s)
        v = acc[:, 2 * hd : 3 * hd] * s
        reached = acc[:, 3 * hd :]
        scores = mm3(split(q), split(k), NT) * scale
        scores = jnp.where(allowed[...] > 0.0, scores, -1e30)
        e = jnp.exp(scores - jnp.max(scores, axis=1, keepdims=True))
        p = e / rowsum(e)
        o = mm(p.astype(BF16), v.astype(BF16)).astype(BF16)
        outs[:, pl.ds(l * hd, hd)] = o
        zo[l, :, pl.ds(3 * hd, hd)] = o
        o32 = o.astype(F32)
        turned = mm(o, diag[l])
        square = square + rowsum(o32 * (2.0 * reached + turned))
        reach = reach + rowsum(o32 * own[:, 6 * hd :].astype(F32))
        q_keep[l] = q
        k_keep[l] = k
        v_keep[l] = v
        p_keep[l] = p
        r_keep[l] = reached + turned
        s_keep[l] = jnp.broadcast_to(s, (s.shape[0], hd))

    s_last = lax.rsqrt(square * inv_width + EPSILON)
    back = s_last * s_last * s_last * inv_width * reach
    factors[layers] = jnp.broadcast_to(back, (back.shape[0], hd)).T[:8]
    factors[layers + 1] = jnp.broadcast_to(s_last, (back.shape[0], hd)).T[:8]
    for l in range(layers):
        grads[:, pl.ds(l * hd, hd)] = s_last * base[place(l)][:, 6 * hd :].astype(F32)

    for l in range(layers - 1, -1, -1):
        d_o = grads[:, pl.ds(l * hd, hd)] - back * r_keep[l]
        p, q, k, v, s = p_keep[l], q_keep[l], k_keep[l], v_keep[l], s_keep[l]
        d_o16 = d_o.astype(BF16)
        d_v = mm(p.astype(BF16), d_o16, TN)
        d_p = mm(d_o16, v.astype(BF16), NT)
        d_s = p * (d_p - rowsum(d_p * p)) * scale
        ds = split(d_s)
        d_q = mm3(ds, split(k))
        d_k = mm3(ds, split(q), TN)
        c = rowsum(d_q * q + d_k * k + d_v * v) * (s[:, 0:1] * s[:, 0:1]) * inv_width
        o32 = outs[:, pl.ds(l * hd, hd)].astype(F32)
        z = jnp.concatenate(
            [rope_back(d_q) * s, rope_back(d_k) * s, d_v * s, -(back * o32)], axis=1
        ).astype(BF16)
        zo[l, :, pl.ds(0, 3 * hd)] = z[:, : 3 * hd]
        factors[l] = jnp.broadcast_to(c, (c.shape[0], hd)).T[:8]
        if l:
            rows = cols[pl.ds(first[l], l)].reshape(l * hd, 4 * hd)
            grads[:, pl.ds(0, l * hd)] += mm(z, rows, NT)
        back = back + c


def scan_layers(pick, blocks, base, stats, cosine, sine, allowed, width):
    layers, _, hd, _ = blocks.shape
    rows = base.shape[1]
    vmem = pl.BlockSpec(memory_space=pltpu.VMEM)
    keep = pltpu.VMEM((layers, rows, hd), F32)
    return pl.pallas_call(
        functools.partial(scan_kernel, layers, width, hd),
        out_shape=(
            jax.ShapeDtypeStruct((layers, rows, 4 * hd), BF16),
            jax.ShapeDtypeStruct((layers + 2, 8, rows), F32),
        ),
        in_specs=[pl.BlockSpec(memory_space=pltpu.SMEM), pl.BlockSpec(memory_space=pl.ANY)] + [vmem] * 5,
        out_specs=(vmem, vmem),
        scratch_shapes=[
            pltpu.VMEM((layers * (layers - 1) // 2, hd, 4 * hd), BF16),
            pltpu.VMEM((layers, hd, hd), BF16),
            pltpu.VMEM((rows, layers * hd), BF16),
            pltpu.VMEM((rows, layers * hd), F32),
            keep, keep, keep, keep, keep, keep,
            pltpu.SemaphoreType.DMA((2, layers)),
            pltpu.SemaphoreType.DMA((layers,)),
        ],
        compiler_params=pltpu.CompilerParams(vmem_limit_bytes=40 * 1024 * 1024),
        cost_estimate=pl.CostEstimate(
            flops=2 * 3 * layers * layers * rows * hd * 4 * hd,
            bytes_accessed=2 * layers * layers * hd * 2 * hd + 4 * layers * rows * 8 * hd,
            transcendentals=layers * rows * rows,
        ),
        name="scan_layers",
    )(pick, blocks, base, stats, cosine, sine, allowed)


def block_kernel(hd, part, order, weights, gain, *refs):
    pieces, out, w, sem = refs[:-3], refs[-3], refs[-2], refs[-1]
    count = w.shape[0]

    def copy(at):
        rows = pl.ds(pl.multiple_of(order[at] * part, part), part)
        return pltpu.make_async_copy(weights.at[rows], w.at[at], sem.at[at])

    for at in range(count):
        copy(at).start()
    first = jnp.zeros((hd, 3 * hd), F32)
    second = jnp.zeros((hd, hd), F32)
    at = 0
    for piece in pieces:
        for i in range(piece.shape[0] // part):
            turned = piece[pl.ds(i * part, part), :].astype(F32).T
            scaled = (turned * gain[pl.ds(order[at], 1), :]).astype(BF16)
            copy(at).wait()
            first = first + mm(scaled, w[at][:, : 3 * hd])
            second = second + mm(turned.astype(BF16), w[at][:, 3 * hd :])
            at += 1
    out[...] = jnp.concatenate([first, second], axis=1).astype(BF16)


def couple(order, weights, gain, pieces):
    hd = weights.shape[1] // 4
    count, part = gain.shape
    vmem = pl.BlockSpec(memory_space=pltpu.VMEM)
    return pl.pallas_call(
        functools.partial(block_kernel, hd, part),
        out_shape=jax.ShapeDtypeStruct((hd, 4 * hd), BF16),
        in_specs=[pl.BlockSpec(memory_space=pltpu.SMEM), pl.BlockSpec(memory_space=pl.ANY)]
        + [vmem] * (1 + len(pieces)),
        out_specs=vmem,
        scratch_shapes=[
            pltpu.VMEM((count, part, 4 * hd), BF16),
            pltpu.SemaphoreType.DMA((count,)),
        ],
        compiler_params=pltpu.CompilerParams(vmem_limit_bytes=48 * 1024 * 1024),
        cost_estimate=pl.CostEstimate(
            flops=2 * weights.size * hd, bytes_accessed=weights.size * 2, transcendentals=0
        ),
        name="couple",
    )(order, weights, gain, *pieces)


def put_term(hd, l, core, h, g, z, o, mine, theirs, first):
    right = mm(g.astype(BF16), o)
    left = mm(h, z)
    term = jnp.concatenate([left, right], axis=1).astype(BF16)
    at = l // 2 - first // 2

    @pl.when((l + core) % 2 == 0)
    def _():
        mine[at] = term

    @pl.when((l + core) % 2 == 1)
    def _():
        theirs[at] = term


def streams(source, target, sems, layers, start):
    def copy(l):
        return pltpu.make_async_copy(source.at[l], target.at[l - start], sems.at[l - start])

    for l in layers:
        copy(l).start()
    return lambda l: copy(l).wait()


def upper_kernel(
    layers, low, hd, pick, w_in, w_out, zo, tokens, factors,
    mine, theirs, h_low, g_out, h_up, held_in, held_out, in_sems, out_sems,
):
    rows = zo.shape[1]
    core = pick[0] % 2
    out_wait = streams(w_out, held_out, out_sems, range(layers), 0)
    in_wait = streams(w_in, held_in, in_sems, range(layers - 1, low - 1, -1), low)
    h = tokens[:, :rows].astype(F32)
    for l in range(layers):
        if l < low:
            h_low[l] = h.astype(BF16)
        else:
            h_up[l - low] = h.astype(BF16)
        out_wait(l)
        h = h + mm(held_out[l], zo[l][:, 3 * hd :], NT)
    g = tokens[:, rows:].astype(F32) * factors[layers + 1][:1] - h * factors[layers][:1]
    for l in range(layers - 1, low - 1, -1):
        z = zo[l][:, : 3 * hd]
        h = h_up[l - low]
        put_term(hd, l, core, h, g, z, zo[l][:, 3 * hd :], mine, theirs, low)
        in_wait(l)
        g = g + (mm(held_in[l - low], z, NT) - h.astype(F32) * factors[l][:1])
    g_out[...] = g


def lower_kernel(
    low, hd, pick, w_in, zo, factors, h_low, g_in,
    mine, theirs, held_in, sems,
):
    core = pick[0] % 2
    wait = streams(w_in, held_in, sems, range(low - 1, 0, -1), 0)
    g = g_in[...]
    for l in range(low - 1, -1, -1):
        z = zo[l][:, : 3 * hd]
        h = h_low[l]
        put_term(hd, l, core, h, g, z, zo[l][:, 3 * hd :], mine, theirs, 0)
        if l:
            wait(l)
            g = g + (mm(held_in[l], z, NT) - h.astype(F32) * factors[l][:1])


def all_terms(pick, w_in, w_out, zo, tokens, factors):
    layers, part, hd = w_out.shape
    rows = zo.shape[1]
    low = 2 * (layers * 3 // 16)
    smem = pl.BlockSpec(memory_space=pltpu.SMEM)
    vmem = pl.BlockSpec(memory_space=pltpu.VMEM)
    far = pl.BlockSpec(memory_space=pl.ANY)
    params = pltpu.CompilerParams(vmem_limit_bytes=48 * 1024 * 1024)
    cost = pl.CostEstimate(
        flops=layers * part * rows * 8 * hd, bytes_accessed=8 * w_out.size, transcendentals=0
    )

    def kind(count):
        return jax.ShapeDtypeStruct((count // 2, part, 4 * hd), BF16)

    upper, upper_out, h_low, g = pl.pallas_call(
        functools.partial(upper_kernel, layers, low, hd),
        out_shape=(
            kind(layers - low),
            kind(layers - low),
            jax.ShapeDtypeStruct((low, part, rows), BF16),
            jax.ShapeDtypeStruct((part, rows), F32),
        ),
        in_specs=[smem, far, far] + [vmem] * 3,
        out_specs=(vmem,) * 4,
        scratch_shapes=[
            pltpu.VMEM((layers - low, part, rows), BF16),
            pltpu.VMEM((layers - low, part, 3 * hd), BF16),
            pltpu.VMEM((layers, part, hd), BF16),
            pltpu.SemaphoreType.DMA((layers - low,)),
            pltpu.SemaphoreType.DMA((layers,)),
        ],
        compiler_params=params,
        cost_estimate=cost,
        name="upper_terms",
    )(pick, w_in, w_out, zo, tokens, factors)
    lower, lower_out = pl.pallas_call(
        functools.partial(lower_kernel, low, hd),
        out_shape=(kind(low), kind(low)),
        in_specs=[smem, far] + [vmem] * 4,
        out_specs=(vmem, vmem),
        scratch_shapes=[
            pltpu.VMEM((low, part, 3 * hd), BF16),
            pltpu.SemaphoreType.DMA((low,)),
        ],
        compiler_params=params,
        cost_estimate=cost,
        name="lower_terms",
    )(pick, w_in, zo, factors, h_low, g)
    return (lower, upper), (lower_out, upper_out)


def moved(block, to):
    n = lax.axis_size("section")
    route = []
    for a in range(n):
        for b in range(n):
            c, d = to(a, b)
            route.append((a * n + b, c * n + d))
    return lax.ppermute(block, ("section", "dp"), route)


def section_move(block):
    return moved(block, lambda a, b: (a ^ b, b))


def dp_move(block):
    return moved(block, lambda a, b: (a, a ^ b))


def swapped(block):
    return moved(block, lambda a, b: (b, a))


def along(block, move):
    n = lax.axis_size("section")
    return lax.ppermute(block, "section", [(i, move(i)) for i in range(n)])


def all_of_dp(block):
    n = lax.axis_size("dp")
    return lax.all_to_all(jnp.broadcast_to(block[None], (n,) + block.shape), "dp", 0, 0)


def across_dp(block):
    n = lax.axis_size("dp")

    def shifted(a, by):
        return lax.ppermute(a, "dp", [(i, (i + 2 * by) % n) for i in range(n)])

    other = lax.ppermute(block, "dp", [(i, i ^ 1) for i in range(n)])
    both = jnp.stack([block, other])
    length = n // 2
    held = [both] + [None] * (length - 1)
    for step in range(1, length // 2 + 1):
        held[step] = shifted(held[step - 1], 1)
        if step < length - step:
            held[length - step] = shifted(held[(length - step + 1) % length], -1)
    return jnp.concatenate(held, axis=0)


def tables(segs, head_size):
    batch, length = segs.shape
    index = jnp.arange(length, dtype=jnp.int32)
    earlier = jnp.sum((segs[:, None, :] < segs[:, :, None]).astype(jnp.int32), axis=-1)
    where_at = (index[None, :] - earlier).astype(F32).reshape(batch * length)
    half = head_size // 2
    freq = ROTARY_BASE ** (-2.0 * jnp.arange(half, dtype=F32) / head_size)
    angle = where_at[:, None] * freq
    cosine, sine = jnp.cos(angle), jnp.sin(angle)
    flat = segs.reshape(batch * length)
    token = jnp.arange(batch * length, dtype=jnp.int32)
    allowed = (
        (flat[:, None] == flat[None, :])
        & (token[:, None] >= token[None, :])
        & (token[:, None] // length == token[None, :] // length)
    )
    return (
        jnp.concatenate([cosine, cosine], axis=-1),
        jnp.concatenate([-sine, sine], axis=-1),
        allowed.astype(F32),
    )


def three(a):
    high = a.astype(BF16)
    rest = a - high.astype(F32)
    middle = rest.astype(BF16)
    return [high, middle, (rest - middle.astype(F32)).astype(BF16)]


def local(x_in, segment_ids, norm_gain, w_attn, final_gain, upstream):
    n = lax.axis_size("section")
    me = lax.axis_index("section")
    row = lax.axis_index("dp")
    micro_count, tok_count, width = x_in.shape
    rows = micro_count * tok_count
    part = width // n
    gain = norm_gain[0].astype(F32)
    last_gain = final_gain.astype(F32)
    weights = w_attn[0]
    hd = weights.shape[1] // 4
    w_in, w_out = weights[:, : 3 * hd], weights[:, 3 * hd :]
    x = x_in.reshape(rows, width)
    up = upstream.reshape(rows, width)

    def cut(a, index, axis=0):
        return lax.dynamic_slice_in_dim(a, index * part, part, axis)

    x32 = x.astype(F32)
    up_gain = up.astype(F32) * last_gain
    first = mm((x32 * gain).astype(BF16), w_in)
    second = mm(jnp.concatenate([x, up_gain.astype(BF16)], axis=0), w_out)
    high, low = split(first[:, : 2 * hd])
    square = jnp.sum(x32 * x32, axis=1, keepdims=True)
    reach = jnp.sum(x32 * up_gain, axis=1, keepdims=True)
    segs = segment_ids.reshape(rows, 1).astype(BF16)
    extra = jnp.concatenate(
        three(square) + three(reach) + [segs, jnp.zeros((rows, hd - 7), BF16)], axis=1
    )
    packed = jnp.concatenate(
        [high, low, first[:, 2 * hd :].astype(BF16), second[:rows].astype(BF16),
         second[rows:].astype(BF16), extra],
        axis=1,
    )
    packed = dp_move(packed)

    pairs = n // 2
    quarter = pairs // 2

    def slot(i):
        return (i % 2) * pairs + i // 2

    def turn(i, x_step, y_step):
        place = i // 2
        across = (place // quarter + x_step) % 2
        along_y = (place % quarter + y_step) % quarter
        return (across * quarter + along_y) * 2 + i % 2

    mine = swapped(cut(weights, slot(row))[:, 3 * hd :])
    near = jnp.concatenate([mine, along(mine, lambda i: turn(i, 1, 0))], axis=0)
    pieces = [near] + [
        along(near, lambda i, k=k: turn(i, 0, k)) for k in range(1, quarter)
    ]
    *pieces, packed = lax.optimization_barrier((*pieces, packed))
    pieces = pieces + [along(p, lambda i: i ^ 1) for p in pieces]
    order = []
    for core in range(2):
        for k in range(quarter):
            for x_step in range(2):
                order.append(slot(turn(me, x_step, -k) ^ core))
    order = jnp.stack(order).astype(jnp.int32)

    w_scaled = (cut(weights, row)[:, : 3 * hd].astype(F32) * cut(gain, row)[:, None]).astype(BF16)
    w_out_all = lax.all_gather(cut(weights, row)[:, 3 * hd :], "section")
    tokens = jnp.concatenate(
        [cut(x, me ^ row, 1).T,
         (cut(up, me ^ row, 1).astype(F32) * cut(last_gain, me ^ row)).astype(BF16).T],
        axis=1,
    )

    block = couple(order, weights, gain.reshape(n, part), pieces)
    returned = swapped(block[:, 2 * hd :])
    on_diag = jnp.concatenate([block[:, 3 * hd :], jnp.zeros((hd, hd), BF16)], axis=1)
    shard = jnp.where(row < me, block[:, : 2 * hd], jnp.where(row == me, on_diag, returned))
    shards = all_of_dp(shard)
    w_scaled, _, _ = lax.optimization_barrier((w_scaled, w_out_all, block))
    w_in_all = lax.all_gather(w_scaled, "section")
    ready, _ = lax.optimization_barrier((shards, w_in_all))
    blocks = lax.all_gather(ready, "section")
    packed, tokens, _ = lax.optimization_barrier((packed, tokens, shards))
    packed = section_move(packed)
    tokens = section_move(dp_move(tokens))
    base = across_dp(packed[:, : 7 * hd])
    tokens, base, blocks = lax.optimization_barrier((tokens, base, blocks))
    extra = packed[:, 7 * hd :].astype(F32)
    stats = jnp.concatenate([rowsum(extra[:, :3]), rowsum(extra[:, 3:6])], axis=1)
    cosine, sine, allowed = tables(
        extra[:, 6].astype(jnp.int32).reshape(micro_count, tok_count), hd
    )

    pick = jnp.stack([me, row]).astype(jnp.int32)
    zo, factors = scan_layers(pick, blocks, base, stats, cosine, sine, allowed, width)

    kept, given = all_terms(pick, w_in_all, w_out_all, zo, tokens, factors)
    mine = jnp.concatenate(
        [
            (k.astype(F32) + along(t, lambda i: i ^ 1).astype(F32)).astype(BF16)
            for k, t in zip(kept, given)
        ],
        axis=0,
    )
    total = lax.psum_scatter(
        mine,
        "section",
        scatter_dimension=0,
        axis_index_groups=[list(range(core, n, 2)) for core in range(2)],
        tiled=True,
    )
    factor = jnp.concatenate(
        [jnp.broadcast_to(cut(gain, row)[:, None], (part, 3 * hd)), jnp.ones((part, hd), F32)], axis=1
    )
    return (total.astype(F32) * factor).astype(BF16)


def solution(mesh):
    placed = (
        P("dp", None, None),
        P("dp", None),
        P("section", None),
        P("section", None, None),
        P(),
        P("dp", None, None),
    )
    return jax.shard_map(
        local, mesh=mesh, in_specs=placed, out_specs=P("section", "dp", None), check_vma=False
    )
```

```python
import functools

import jax
import jax.numpy as jnp
from jax import lax
from jax.experimental import pallas as pl
from jax.experimental.pallas import tpu as pltpu
from jax.sharding import PartitionSpec as P

EPSILON = 1e-05
ROTARY_BASE = 500000.0
F32 = jnp.float32
BF16 = jnp.bfloat16
NN = (((1,), (0,)), ((), ()))
NT = (((1,), (1,)), ((), ()))
TN = (((0,), (0,)), ((), ()))


def mm(a, b, dims=NN):
    return lax.dot_general(a, b, dims, preferred_element_type=F32)


def split(a):
    high = a.astype(BF16)
    return high, (a - high.astype(F32)).astype(BF16)


def mm3(a, b, dims=NN):
    (ah, al), (bh, bl) = a, b
    ((i,), (j,)), _ = dims
    both = mm(jnp.concatenate([ah, al], axis=i), jnp.concatenate([bh, bh], axis=j), dims)
    return both + mm(ah, bl, dims)


def rowsum(a):
    return jnp.sum(a, axis=1, keepdims=True)


def scan_kernel(
    layers, width, hd,
    pick, blocks, base, stats, cosine, sine, allowed,
    zo, factors,
    cols, diag, outs, grads, q_keep, k_keep, v_keep, p_keep, r_keep, s_keep, col_sem, diag_sem,
):
    first = [l * (l - 1) // 2 for l in range(layers + 1)]

    def copies(l):
        span = pl.ds(first[l], l)
        return (
            pltpu.make_async_copy(
                blocks.at[l, pl.ds(0, l)], cols.at[span, :, pl.ds(0, 2 * hd)], col_sem.at[0, l]
            ),
            pltpu.make_async_copy(
                blocks.at[pl.ds(0, l), l], cols.at[span, :, pl.ds(2 * hd, 2 * hd)], col_sem.at[1, l]
            ),
        )

    def diag_copy(l):
        return pltpu.make_async_copy(blocks.at[l, l, :, pl.ds(0, hd)], diag.at[l], diag_sem.at[l])

    for l in range(layers):
        diag_copy(l).start()
    for l in range(1, layers):
        for c in copies(l):
            c.start()

    def place(l):
        c = pick[0] ^ l
        return ((pick[1] // 2 + layers // 2 - c // 2) % (layers // 2)) * 2 + ((c ^ pick[1]) & 1)

    cosine, sine = cosine[...], sine[...]
    shut = allowed[...] == 0.0

    def rope(u):
        return u * cosine + pltpu.roll(u, hd // 2, 1) * sine

    def rope_back(w):
        return w * cosine - pltpu.roll(w, hd // 2, 1) * sine

    def start_of(l):
        own = base[place(l)]
        return jnp.concatenate(
            [
                own[:, : 2 * hd].astype(F32) + own[:, 2 * hd : 4 * hd].astype(F32),
                own[:, 4 * hd : 6 * hd].astype(F32),
            ],
            axis=1,
        )

    scale = hd ** (-0.5)
    inv_width = 1.0 / width
    square = stats[:, 0:1]
    reach = stats[:, 1:2]
    o = None
    early = layers // 3
    partial = start_of(0)
    for l in range(layers):
        if l in (0, early):
            for i in range(1, early + 1) if l == 0 else range(early + 1, layers):
                for c in copies(i):
                    c.wait()
            for i in range(early) if l == 0 else range(early, layers):
                diag_copy(i).wait()
        acc = partial
        if l:
            acc = acc + mm(o, cols[first[l] + l - 1])
        s = lax.rsqrt(square * inv_width + EPSILON)
        q = rope(acc[:, :hd] * s)
        k = rope(acc[:, hd : 2 * hd] * s)
        v = acc[:, 2 * hd : 3 * hd] * s
        reached = acc[:, 3 * hd :]
        scores = mm3(split(q), split(k), NT) * scale
        if l + 1 < layers:
            partial = start_of(l + 1)
            if l:
                rows = cols[pl.ds(first[l + 1], l)].reshape(l * hd, 4 * hd)
                partial = partial + mm(outs[:, pl.ds(0, l * hd)], rows)
        scores = jnp.where(shut, -1e30, scores)
        e = jnp.exp(scores - jnp.max(scores, axis=1, keepdims=True))
        inverse = 1.0 / rowsum(e)
        o = (mm(e.astype(BF16), v.astype(BF16)) * inverse).astype(BF16)
        outs[:, pl.ds(l * hd, hd)] = o
        zo[l, :, pl.ds(3 * hd, hd)] = o
        o32 = o.astype(F32)
        turned = mm(o, diag[l])
        square = square + rowsum(o32 * (2.0 * reached + turned))
        reach = reach + rowsum(o32 * base[place(l)][:, 6 * hd :].astype(F32))
        q_keep[l] = q
        k_keep[l] = k
        v_keep[l] = v
        p_keep[l] = e * inverse
        r_keep[l] = reached + turned
        s_keep[l] = jnp.broadcast_to(s, (s.shape[0], hd))

    s_last = lax.rsqrt(square * inv_width + EPSILON)
    back = s_last * s_last * s_last * inv_width * reach
    factors[layers] = jnp.broadcast_to(back, (back.shape[0], hd)).T[:8]
    factors[layers + 1] = jnp.broadcast_to(s_last, (back.shape[0], hd)).T[:8]
    for l in range(layers):
        grads[:, pl.ds(l * hd, hd)] = s_last * base[place(l)][:, 6 * hd :].astype(F32)

    waiting = None
    for l in range(layers - 1, -1, -1):
        d_o = grads[:, pl.ds(l * hd, hd)] - back * r_keep[l]
        if waiting is not None:
            d_o = d_o + mm(waiting, cols[first[l + 1] + l], NT)
        p, q, k, v, s = p_keep[l], q_keep[l], k_keep[l], v_keep[l], s_keep[l]
        d_o16 = d_o.astype(BF16)
        d_p = mm(d_o16, v.astype(BF16), NT)
        d_v = mm(p.astype(BF16), d_o16, TN)
        if waiting is not None and l:
            rows = cols[pl.ds(first[l + 1], l)].reshape(l * hd, 4 * hd)
            grads[:, pl.ds(0, l * hd)] += mm(waiting, rows, NT)
        d_s = p * (d_p - rowsum(d_p * p)) * scale
        ds = split(d_s)
        d_q = mm3(ds, split(k))
        d_k = mm3(ds, split(q), TN)
        c = rowsum(d_q * q + d_k * k + d_v * v) * (s[:, 0:1] * s[:, 0:1]) * inv_width
        o32 = outs[:, pl.ds(l * hd, hd)].astype(F32)
        z = jnp.concatenate(
            [rope_back(d_q) * s, rope_back(d_k) * s, d_v * s, -(back * o32)], axis=1
        ).astype(BF16)
        zo[l, :, pl.ds(0, 3 * hd)] = z[:, : 3 * hd]
        factors[l] = jnp.broadcast_to(c, (c.shape[0], hd)).T[:8]
        waiting = z
        back = back + c


def scan_layers(pick, blocks, base, stats, cosine, sine, allowed, width):
    layers, _, hd, _ = blocks.shape
    rows = base.shape[1]
    vmem = pl.BlockSpec(memory_space=pltpu.VMEM)
    keep = pltpu.VMEM((layers, rows, hd), F32)
    return pl.pallas_call(
        functools.partial(scan_kernel, layers, width, hd),
        out_shape=(
            jax.ShapeDtypeStruct((layers, rows, 4 * hd), BF16),
            jax.ShapeDtypeStruct((layers + 2, 8, rows), F32),
        ),
        in_specs=[pl.BlockSpec(memory_space=pltpu.SMEM), pl.BlockSpec(memory_space=pl.ANY)] + [vmem] * 5,
        out_specs=(vmem, vmem),
        scratch_shapes=[
            pltpu.VMEM((layers * (layers - 1) // 2, hd, 4 * hd), BF16),
            pltpu.VMEM((layers, hd, hd), BF16),
            pltpu.VMEM((rows, layers * hd), BF16),
            pltpu.VMEM((rows, layers * hd), F32),
            keep, keep, keep, keep, keep, keep,
            pltpu.SemaphoreType.DMA((2, layers)),
            pltpu.SemaphoreType.DMA((layers,)),
        ],
        compiler_params=pltpu.CompilerParams(vmem_limit_bytes=40 * 1024 * 1024),
        cost_estimate=pl.CostEstimate(
            flops=2 * 3 * layers * layers * rows * hd * 4 * hd,
            bytes_accessed=2 * layers * layers * hd * 2 * hd + 4 * layers * rows * 8 * hd,
            transcendentals=layers * rows * rows,
        ),
        name="scan_layers",
    )(pick, blocks, base, stats, cosine, sine, allowed)


def block_kernel(hd, part, order, weights, gain, *refs):
    pieces, out, w, sem = refs[:-3], refs[-3], refs[-2], refs[-1]
    count = w.shape[0]

    def copy(at):
        rows = pl.ds(pl.multiple_of(order[at] * part, part), part)
        return pltpu.make_async_copy(weights.at[rows], w.at[at], sem.at[at])

    for at in range(count):
        copy(at).start()
    first = jnp.zeros((hd, 3 * hd), F32)
    second = jnp.zeros((hd, hd), F32)
    at = 0
    for piece in pieces:
        for i in range(piece.shape[0] // part):
            turned = piece[pl.ds(i * part, part), :].astype(F32).T
            scaled = (turned * gain[pl.ds(order[at], 1), :]).astype(BF16)
            copy(at).wait()
            first = first + mm(scaled, w[at][:, : 3 * hd])
            second = second + mm(turned.astype(BF16), w[at][:, 3 * hd :])
            at += 1
    out[...] = jnp.concatenate([first, second], axis=1).astype(BF16)


def couple(order, weights, gain, pieces):
    hd = weights.shape[1] // 4
    count, part = gain.shape
    vmem = pl.BlockSpec(memory_space=pltpu.VMEM)
    return pl.pallas_call(
        functools.partial(block_kernel, hd, part),
        out_shape=jax.ShapeDtypeStruct((hd, 4 * hd), BF16),
        in_specs=[pl.BlockSpec(memory_space=pltpu.SMEM), pl.BlockSpec(memory_space=pl.ANY)]
        + [vmem] * (1 + len(pieces)),
        out_specs=vmem,
        scratch_shapes=[
            pltpu.VMEM((count, part, 4 * hd), BF16),
            pltpu.SemaphoreType.DMA((count,)),
        ],
        compiler_params=pltpu.CompilerParams(vmem_limit_bytes=48 * 1024 * 1024),
        cost_estimate=pl.CostEstimate(
            flops=2 * weights.size * hd, bytes_accessed=weights.size * 2, transcendentals=0
        ),
        name="couple",
    )(order, weights, gain, *pieces)


def put_terms(hd, first, zo, hs, gs, out):
    for i in range(out.shape[0]):
        l = 2 * i + first
        z = zo[l]
        out[i, :, pl.ds(0, 3 * hd)] = mm(hs[l], z[:, : 3 * hd]).astype(BF16)
        out[i, :, pl.ds(3 * hd, hd)] = mm(gs[l], z[:, 3 * hd :]).astype(BF16)


def hidden_kernel(layers, hd, w_out, zo, tokens, hs):
    rows = zo.shape[1]
    h = tokens[:, :rows].astype(F32)
    for l in range(layers):
        hs[l] = h.astype(BF16)
        h = h + mm(w_out[l], zo[l][:, 3 * hd :], NT)
    hs[layers] = h.astype(BF16)


def grad_kernel(layers, hd, w_in, zo, tokens, factors, hs, gs):
    rows = zo.shape[1]
    g = (
        tokens[:, rows:].astype(F32) * factors[layers + 1][:1]
        - hs[layers].astype(F32) * factors[layers][:1]
    )
    for l in range(layers - 1, -1, -1):
        gs[l] = g.astype(BF16)
        if l:
            z = zo[l]
            g = g + (mm(w_in[l], z[:, : 3 * hd], NT) - hs[l].astype(F32) * factors[l][:1])


def term_kernel(hd, first, zo, hs, gs, out):
    put_terms(hd, first[0], zo, hs, gs, out)


def all_terms(pick, w_in, w_out, zo, tokens, factors):
    layers, part, hd = w_out.shape
    rows = zo.shape[1]
    smem = pl.BlockSpec(memory_space=pltpu.SMEM)
    vmem = pl.BlockSpec(memory_space=pltpu.VMEM)
    params = pltpu.CompilerParams(vmem_limit_bytes=32 * 1024 * 1024)
    cost = pl.CostEstimate(
        flops=layers * part * rows * 8 * hd, bytes_accessed=8 * w_out.size, transcendentals=0
    )
    kind = jax.ShapeDtypeStruct((layers // 2, part, 4 * hd), BF16)
    hs = pl.pallas_call(
        functools.partial(hidden_kernel, layers, hd),
        out_shape=jax.ShapeDtypeStruct((layers + 1, part, rows), BF16),
        in_specs=[vmem] * 3,
        out_specs=vmem,
        compiler_params=params,
        cost_estimate=cost,
        name="hidden_states",
    )(w_out, zo, tokens)
    gs = pl.pallas_call(
        functools.partial(grad_kernel, layers, hd),
        out_shape=jax.ShapeDtypeStruct((layers, part, rows), BF16),
        in_specs=[vmem] * 5,
        out_specs=vmem,
        compiler_params=params,
        cost_estimate=cost,
        name="state_grads",
    )(w_in, zo, tokens, factors, hs)
    terms = pl.pallas_call(
        functools.partial(term_kernel, hd),
        out_shape=kind,
        in_specs=[smem, vmem, vmem, vmem],
        out_specs=vmem,
        compiler_params=pltpu.CompilerParams(vmem_limit_bytes=32 * 1024 * 1024),
        cost_estimate=cost,
        name="terms",
    )
    core = pick[:1] % 2
    theirs = terms(1 - core, zo, hs, gs)
    return terms(core, zo, hs, gs), theirs


def moved(block, to):
    n = lax.axis_size("section")
    route = []
    for a in range(n):
        for b in range(n):
            c, d = to(a, b)
            route.append((a * n + b, c * n + d))
    return lax.ppermute(block, ("section", "dp"), route)


def section_move(block):
    return moved(block, lambda a, b: (a ^ b, b))


def dp_move(block):
    return moved(block, lambda a, b: (a, a ^ b))


def swapped(block):
    return moved(block, lambda a, b: (b, a))


def along(block, move):
    n = lax.axis_size("section")
    return lax.ppermute(block, "section", [(i, move(i)) for i in range(n)])


def all_of_dp(block):
    n = lax.axis_size("dp")
    return lax.all_to_all(jnp.broadcast_to(block[None], (n,) + block.shape), "dp", 0, 0)


def across_dp(block):
    n = lax.axis_size("dp")

    def shifted(a, by):
        return lax.ppermute(a, "dp", [(i, (i + 2 * by) % n) for i in range(n)])

    other = lax.ppermute(block, "dp", [(i, i ^ 1) for i in range(n)])
    both = jnp.stack([block, other])
    length = n // 2
    held = [both] + [None] * (length - 1)
    for step in range(1, length // 2 + 1):
        held[step] = shifted(held[step - 1], 1)
        if step < length - step:
            held[length - step] = shifted(held[(length - step + 1) % length], -1)
    return jnp.concatenate(held, axis=0)


def tables(segs, head_size):
    batch, length = segs.shape
    index = jnp.arange(length, dtype=jnp.int32)
    earlier = jnp.sum((segs[:, None, :] < segs[:, :, None]).astype(jnp.int32), axis=-1)
    where_at = (index[None, :] - earlier).astype(F32).reshape(batch * length)
    half = head_size // 2
    freq = ROTARY_BASE ** (-2.0 * jnp.arange(half, dtype=F32) / head_size)
    angle = where_at[:, None] * freq
    cosine, sine = jnp.cos(angle), jnp.sin(angle)
    flat = segs.reshape(batch * length)
    token = jnp.arange(batch * length, dtype=jnp.int32)
    allowed = (
        (flat[:, None] == flat[None, :])
        & (token[:, None] >= token[None, :])
        & (token[:, None] // length == token[None, :] // length)
    )
    return (
        jnp.concatenate([cosine, cosine], axis=-1),
        jnp.concatenate([-sine, sine], axis=-1),
        allowed.astype(F32),
    )


def three(a):
    high = a.astype(BF16)
    rest = a - high.astype(F32)
    middle = rest.astype(BF16)
    return [high, middle, (rest - middle.astype(F32)).astype(BF16)]


def local(x_in, segment_ids, norm_gain, w_attn, final_gain, upstream):
    n = lax.axis_size("section")
    me = lax.axis_index("section")
    row = lax.axis_index("dp")
    micro_count, tok_count, width = x_in.shape
    rows = micro_count * tok_count
    part = width // n
    gain = norm_gain[0].astype(F32)
    last_gain = final_gain.astype(F32)
    weights = w_attn[0]
    hd = weights.shape[1] // 4
    w_in, w_out = weights[:, : 3 * hd], weights[:, 3 * hd :]
    x = x_in.reshape(rows, width)
    up = upstream.reshape(rows, width)

    def cut(a, index, axis=0):
        return lax.dynamic_slice_in_dim(a, index * part, part, axis)

    x32 = x.astype(F32)
    up_gain = up.astype(F32) * last_gain
    first = mm((x32 * gain).astype(BF16), w_in)
    second = mm(jnp.concatenate([x, up_gain.astype(BF16)], axis=0), w_out)
    high, low = split(first[:, : 2 * hd])
    square = jnp.sum(x32 * x32, axis=1, keepdims=True)
    reach = jnp.sum(x32 * up_gain, axis=1, keepdims=True)
    segs = segment_ids.reshape(rows, 1).astype(BF16)
    extra = jnp.concatenate(
        three(square) + three(reach) + [segs, jnp.zeros((rows, hd - 7), BF16)], axis=1
    )
    packed = jnp.concatenate(
        [high, low, first[:, 2 * hd :].astype(BF16), second[:rows].astype(BF16),
         second[rows:].astype(BF16), extra],
        axis=1,
    )
    packed = dp_move(packed)

    pairs = n // 2
    quarter = pairs // 2

    def slot(i):
        return (i % 2) * pairs + i // 2

    def turn(i, x_step, y_step):
        place = i // 2
        across = (place // quarter + x_step) % 2
        along_y = (place % quarter + y_step) % quarter
        return (across * quarter + along_y) * 2 + i % 2

    mine = swapped(cut(weights, slot(row))[:, 3 * hd :])
    near = jnp.concatenate([mine, along(mine, lambda i: turn(i, 1, 0))], axis=0)
    pieces = [near] + [
        along(near, lambda i, k=k: turn(i, 0, k)) for k in range(1, quarter)
    ]
    *pieces, packed = lax.optimization_barrier((*pieces, packed))
    pieces = pieces + [along(p, lambda i: i ^ 1) for p in pieces]
    order = []
    for core in range(2):
        for k in range(quarter):
            for x_step in range(2):
                order.append(slot(turn(me, x_step, -k) ^ core))
    order = jnp.stack(order).astype(jnp.int32)

    w_scaled = (cut(weights, row)[:, : 3 * hd].astype(F32) * cut(gain, row)[:, None]).astype(BF16)
    w_out_all = lax.all_gather(cut(weights, row)[:, 3 * hd :], "section")
    w_scaled, _, _ = lax.optimization_barrier((w_scaled, w_out_all, pieces[-1]))
    w_in_all = lax.all_gather(w_scaled, "section")
    tokens = jnp.concatenate(
        [cut(x, me ^ row, 1).T,
         (cut(up, me ^ row, 1).astype(F32) * cut(last_gain, me ^ row)).astype(BF16).T],
        axis=1,
    )

    block = couple(order, weights, gain.reshape(n, part), pieces)
    returned = swapped(block[:, 2 * hd :])
    on_diag = jnp.concatenate([block[:, 3 * hd :], jnp.zeros((hd, hd), BF16)], axis=1)
    shard = jnp.where(row < me, block[:, : 2 * hd], jnp.where(row == me, on_diag, returned))
    shards = all_of_dp(shard)
    ready, _ = lax.optimization_barrier((shards, w_in_all))
    blocks = lax.all_gather(ready, "section")
    packed, tokens, _ = lax.optimization_barrier((packed, tokens, shards))
    packed = section_move(packed)
    tokens = section_move(dp_move(tokens))
    base = across_dp(packed[:, : 7 * hd])
    tokens, base, blocks = lax.optimization_barrier((tokens, base, blocks))
    extra = packed[:, 7 * hd :].astype(F32)
    stats = jnp.concatenate([rowsum(extra[:, :3]), rowsum(extra[:, 3:6])], axis=1)
    cosine, sine, allowed = tables(
        extra[:, 6].astype(jnp.int32).reshape(micro_count, tok_count), hd
    )

    pick = jnp.stack([me, row]).astype(jnp.int32)
    zo, factors = scan_layers(pick, blocks, base, stats, cosine, sine, allowed, width)

    mine, theirs = all_terms(pick, w_in_all, w_out_all, zo, tokens, factors)
    theirs = along(theirs, lambda i: i ^ 1)
    mine = (mine.astype(F32) + theirs.astype(F32)).astype(BF16)
    total = lax.psum_scatter(
        mine,
        "section",
        scatter_dimension=0,
        axis_index_groups=[list(range(core, n, 2)) for core in range(2)],
        tiled=True,
    )
    factor = jnp.concatenate(
        [jnp.broadcast_to(cut(gain, row)[:, None], (part, 3 * hd)), jnp.ones((part, hd), F32)], axis=1
    )
    return (total.astype(F32) * factor).astype(BF16)


def solution(mesh):
    placed = (
        P("dp", None, None),
        P("dp", None),
        P("section", None),
        P("section", None, None),
        P(),
        P("dp", None, None),
    )
    return jax.shard_map(
        local, mesh=mesh, in_specs=placed, out_specs=P("section", "dp", None), check_vma=False
    )
```

```python
import functools

import jax
import jax.numpy as jnp
from jax import lax
from jax.experimental import pallas as pl
from jax.experimental.pallas import tpu as pltpu
from jax.sharding import PartitionSpec as P

EPSILON = 1e-05
ROTARY_BASE = 500000.0
F32 = jnp.float32
BF16 = jnp.bfloat16
NN = (((1,), (0,)), ((), ()))
NT = (((1,), (1,)), ((), ()))
TN = (((0,), (0,)), ((), ()))


def mm(a, b, dims=NN):
    return lax.dot_general(a, b, dims, preferred_element_type=F32)


def split(a):
    high = a.astype(BF16)
    return high, (a - high.astype(F32)).astype(BF16)


def mm3(a, b, dims=NN):
    (ah, al), (bh, bl) = a, b
    ((i,), (j,)), _ = dims
    both = mm(jnp.concatenate([ah, al], axis=i), jnp.concatenate([bh, bh], axis=j), dims)
    return both + mm(ah, bl, dims)


def rowsum(a):
    return jnp.sum(a, axis=1, keepdims=True)


def scan_kernel(
    layers, width, hd,
    pick, blocks, base, stats, cosine, sine, allowed,
    zo, factors,
    cols, diag, outs, grads, q_keep, k_keep, v_keep, p_keep, r_keep, s_keep, col_sem, diag_sem,
):
    first = [l * (l - 1) // 2 for l in range(layers + 1)]

    def copies(l):
        span = pl.ds(first[l], l)
        return (
            pltpu.make_async_copy(
                blocks.at[l, pl.ds(0, l)], cols.at[span, :, pl.ds(0, 2 * hd)], col_sem.at[0, l]
            ),
            pltpu.make_async_copy(
                blocks.at[pl.ds(0, l), l], cols.at[span, :, pl.ds(2 * hd, 2 * hd)], col_sem.at[1, l]
            ),
        )

    def diag_copy(l):
        return pltpu.make_async_copy(blocks.at[l, l, :, pl.ds(0, hd)], diag.at[l], diag_sem.at[l])

    for l in range(layers):
        diag_copy(l).start()
    for l in range(1, layers):
        for c in copies(l):
            c.start()

    def place(l):
        c = pick[0] ^ l
        return ((pick[1] // 2 + layers // 2 - c // 2) % (layers // 2)) * 2 + ((c ^ pick[1]) & 1)

    cosine, sine = cosine[...], sine[...]
    shut = allowed[...] == 0.0

    def rope(u):
        return u * cosine + pltpu.roll(u, hd // 2, 1) * sine

    def rope_back(w):
        return w * cosine - pltpu.roll(w, hd // 2, 1) * sine

    def start_of(l):
        own = base[place(l)]
        return jnp.concatenate(
            [
                own[:, : 2 * hd].astype(F32) + own[:, 2 * hd : 4 * hd].astype(F32),
                own[:, 4 * hd : 6 * hd].astype(F32),
            ],
            axis=1,
        )

    scale = hd ** (-0.5)
    inv_width = 1.0 / width
    square = stats[:, 0:1]
    reach = stats[:, 1:2]
    o = None
    early = layers // 3
    partial = start_of(0)
    for l in range(layers):
        if l in (0, early):
            for i in range(1, early + 1) if l == 0 else range(early + 1, layers):
                for c in copies(i):
                    c.wait()
            for i in range(early) if l == 0 else range(early, layers):
                diag_copy(i).wait()
        acc = partial
        if l:
            acc = acc + mm(o, cols[first[l] + l - 1])
        s = lax.rsqrt(square * inv_width + EPSILON)
        q = rope(acc[:, :hd] * s)
        k = rope(acc[:, hd : 2 * hd] * s)
        v = acc[:, 2 * hd : 3 * hd] * s
        reached = acc[:, 3 * hd :]
        scores = mm3(split(q), split(k), NT) * scale
        if l + 1 < layers:
            partial = start_of(l + 1)
            if l:
                rows = cols[pl.ds(first[l + 1], l)].reshape(l * hd, 4 * hd)
                partial = partial + mm(outs[:, pl.ds(0, l * hd)], rows)
        scores = jnp.where(shut, -1e30, scores)
        e = jnp.exp(scores - jnp.max(scores, axis=1, keepdims=True))
        inverse = 1.0 / rowsum(e)
        o = (mm(e.astype(BF16), v.astype(BF16)) * inverse).astype(BF16)
        outs[:, pl.ds(l * hd, hd)] = o
        zo[l, :, pl.ds(3 * hd, hd)] = o
        o32 = o.astype(F32)
        turned = mm(o, diag[l])
        square = jnp.maximum(square + rowsum(o32 * (2.0 * reached + turned)), 0.0)
        reach = reach + rowsum(o32 * base[place(l)][:, 6 * hd :].astype(F32))
        q_keep[l] = q
        k_keep[l] = k
        v_keep[l] = v
        p_keep[l] = e * inverse
        r_keep[l] = reached + turned
        s_keep[l] = jnp.broadcast_to(s, (s.shape[0], hd))

    s_last = lax.rsqrt(square * inv_width + EPSILON)
    back = s_last * s_last * s_last * inv_width * reach
    factors[layers] = jnp.broadcast_to(back, (back.shape[0], hd)).T[:8]
    factors[layers + 1] = jnp.broadcast_to(s_last, (back.shape[0], hd)).T[:8]
    for l in range(layers):
        grads[:, pl.ds(l * hd, hd)] = s_last * base[place(l)][:, 6 * hd :].astype(F32)

    waiting = None
    for l in range(layers - 1, -1, -1):
        d_o = grads[:, pl.ds(l * hd, hd)] - back * r_keep[l]
        if waiting is not None:
            d_o = d_o + mm(waiting, cols[first[l + 1] + l], NT)
        p, q, k, v, s = p_keep[l], q_keep[l], k_keep[l], v_keep[l], s_keep[l]
        d_o16 = d_o.astype(BF16)
        d_p = mm(d_o16, v.astype(BF16), NT)
        d_v = mm(p.astype(BF16), d_o16, TN)
        if waiting is not None and l:
            rows = cols[pl.ds(first[l + 1], l)].reshape(l * hd, 4 * hd)
            grads[:, pl.ds(0, l * hd)] += mm(waiting, rows, NT)
        d_s = p * (d_p - rowsum(d_p * p)) * scale
        ds = split(d_s)
        d_q = mm3(ds, split(k))
        d_k = mm3(ds, split(q), TN)
        c = rowsum(d_q * q + d_k * k + d_v * v) * (s[:, 0:1] * s[:, 0:1]) * inv_width
        o32 = outs[:, pl.ds(l * hd, hd)].astype(F32)
        z = jnp.concatenate(
            [rope_back(d_q) * s, rope_back(d_k) * s, d_v * s, -(back * o32)], axis=1
        ).astype(BF16)
        zo[l, :, pl.ds(0, 3 * hd)] = z[:, : 3 * hd]
        factors[l] = jnp.broadcast_to(c, (c.shape[0], hd)).T[:8]
        waiting = z
        back = back + c


def scan_layers(pick, blocks, base, stats, cosine, sine, allowed, width):
    layers, _, hd, _ = blocks.shape
    rows = base.shape[1]
    vmem = pl.BlockSpec(memory_space=pltpu.VMEM)
    keep = pltpu.VMEM((layers, rows, hd), F32)
    return pl.pallas_call(
        functools.partial(scan_kernel, layers, width, hd),
        out_shape=(
            jax.ShapeDtypeStruct((layers, rows, 4 * hd), BF16),
            jax.ShapeDtypeStruct((layers + 2, 8, rows), F32),
        ),
        in_specs=[pl.BlockSpec(memory_space=pltpu.SMEM), pl.BlockSpec(memory_space=pl.ANY)] + [vmem] * 5,
        out_specs=(vmem, vmem),
        scratch_shapes=[
            pltpu.VMEM((layers * (layers - 1) // 2, hd, 4 * hd), BF16),
            pltpu.VMEM((layers, hd, hd), BF16),
            pltpu.VMEM((rows, layers * hd), BF16),
            pltpu.VMEM((rows, layers * hd), F32),
            keep, keep, keep, keep, keep, keep,
            pltpu.SemaphoreType.DMA((2, layers)),
            pltpu.SemaphoreType.DMA((layers,)),
        ],
        compiler_params=pltpu.CompilerParams(vmem_limit_bytes=40 * 1024 * 1024),
        cost_estimate=pl.CostEstimate(
            flops=2 * 3 * layers * layers * rows * hd * 4 * hd,
            bytes_accessed=2 * layers * layers * hd * 2 * hd + 4 * layers * rows * 8 * hd,
            transcendentals=layers * rows * rows,
        ),
        name="scan_layers",
    )(pick, blocks, base, stats, cosine, sine, allowed)


def block_kernel(hd, part, order, weights, gain, start, *refs):
    pieces, out, w, sem = refs[:-3], refs[-3], refs[-2], refs[-1]
    count = w.shape[0]

    def copy(at):
        rows = pl.ds(pl.multiple_of(order[at] * part, part), part)
        return pltpu.make_async_copy(weights.at[rows], w.at[at], sem.at[at])

    for at in range(count):
        copy(at).start()
    first = start[:, : 3 * hd]
    second = start[:, 3 * hd :]
    at = 0
    for piece in pieces:
        for i in range(piece.shape[0] // part):
            turned = piece[pl.ds(i * part, part), :].astype(F32).T
            scaled = (turned * gain[pl.ds(order[at], 1), :]).astype(BF16)
            copy(at).wait()
            first = first + mm(scaled, w[at][:, : 3 * hd])
            second = second + mm(turned.astype(BF16), w[at][:, 3 * hd :])
            at += 1
    out[...] = jnp.concatenate([first, second], axis=1).astype(out.dtype)


def couple(order, weights, gain, start, pieces, kind):
    hd = weights.shape[1] // 4
    count, part = order.shape[0], gain.shape[1]
    vmem = pl.BlockSpec(memory_space=pltpu.VMEM)
    return pl.pallas_call(
        functools.partial(block_kernel, hd, part),
        out_shape=jax.ShapeDtypeStruct((hd, 4 * hd), kind),
        in_specs=[pl.BlockSpec(memory_space=pltpu.SMEM), pl.BlockSpec(memory_space=pl.ANY)]
        + [vmem] * (2 + len(pieces)),
        out_specs=vmem,
        scratch_shapes=[
            pltpu.VMEM((count, part, 4 * hd), BF16),
            pltpu.SemaphoreType.DMA((count,)),
        ],
        compiler_params=pltpu.CompilerParams(vmem_limit_bytes=48 * 1024 * 1024),
        cost_estimate=pl.CostEstimate(
            flops=2 * weights.size * hd, bytes_accessed=weights.size * 2, transcendentals=0
        ),
        name="couple",
    )(order, weights, gain, start, *pieces)


def put_terms(hd, first, zo, hs, gs, out):
    for i in range(out.shape[0]):
        l = 2 * i + first
        z = zo[l]
        out[i, :, pl.ds(0, 3 * hd)] = mm(hs[l], z[:, : 3 * hd]).astype(BF16)
        out[i, :, pl.ds(3 * hd, hd)] = mm(gs[l], z[:, 3 * hd :]).astype(BF16)


def hidden_kernel(layers, hd, w_out, zo, tokens, hs):
    rows = zo.shape[1]
    h = tokens[:, :rows].astype(F32)
    for l in range(layers):
        hs[l] = h.astype(BF16)
        h = h + mm(w_out[l], zo[l][:, 3 * hd :], NT)
    hs[layers] = h.astype(BF16)


def grad_kernel(layers, hd, w_in, zo, tokens, factors, hs, gs):
    rows = zo.shape[1]
    g = (
        tokens[:, rows:].astype(F32) * factors[layers + 1][:1]
        - hs[layers].astype(F32) * factors[layers][:1]
    )
    for l in range(layers - 1, -1, -1):
        gs[l] = g.astype(BF16)
        if l:
            z = zo[l]
            g = g + (mm(w_in[l], z[:, : 3 * hd], NT) - hs[l].astype(F32) * factors[l][:1])


def term_kernel(hd, first, zo, hs, gs, out):
    put_terms(hd, first[0], zo, hs, gs, out)


def all_terms(pick, w_in, w_out, zo, tokens, factors):
    layers, part, hd = w_out.shape
    rows = zo.shape[1]
    smem = pl.BlockSpec(memory_space=pltpu.SMEM)
    vmem = pl.BlockSpec(memory_space=pltpu.VMEM)
    params = pltpu.CompilerParams(vmem_limit_bytes=32 * 1024 * 1024)
    cost = pl.CostEstimate(
        flops=layers * part * rows * 8 * hd, bytes_accessed=8 * w_out.size, transcendentals=0
    )
    kind = jax.ShapeDtypeStruct((layers // 2, part, 4 * hd), BF16)
    hs = pl.pallas_call(
        functools.partial(hidden_kernel, layers, hd),
        out_shape=jax.ShapeDtypeStruct((layers + 1, part, rows), BF16),
        in_specs=[vmem] * 3,
        out_specs=vmem,
        compiler_params=params,
        cost_estimate=cost,
        name="hidden_states",
    )(w_out, zo, tokens)
    gs = pl.pallas_call(
        functools.partial(grad_kernel, layers, hd),
        out_shape=jax.ShapeDtypeStruct((layers, part, rows), BF16),
        in_specs=[vmem] * 5,
        out_specs=vmem,
        compiler_params=params,
        cost_estimate=cost,
        name="state_grads",
    )(w_in, zo, tokens, factors, hs)
    terms = pl.pallas_call(
        functools.partial(term_kernel, hd),
        out_shape=kind,
        in_specs=[smem, vmem, vmem, vmem],
        out_specs=vmem,
        compiler_params=pltpu.CompilerParams(vmem_limit_bytes=32 * 1024 * 1024),
        cost_estimate=cost,
        name="terms",
    )
    core = pick[:1] % 2
    theirs = terms(1 - core, zo, hs, gs)
    return terms(core, zo, hs, gs), theirs


def moved(block, to):
    n = lax.axis_size("section")
    route = []
    for a in range(n):
        for b in range(n):
            c, d = to(a, b)
            route.append((a * n + b, c * n + d))
    return lax.ppermute(block, ("section", "dp"), route)


def section_move(block):
    return moved(block, lambda a, b: (a ^ b, b))


def dp_move(block):
    return moved(block, lambda a, b: (a, a ^ b))


def swapped(block):
    return moved(block, lambda a, b: (b, a))


def along(block, move):
    n = lax.axis_size("section")
    return lax.ppermute(block, "section", [(i, move(i)) for i in range(n)])


def all_of_dp(block):
    n = lax.axis_size("dp")
    return lax.all_to_all(jnp.broadcast_to(block[None], (n,) + block.shape), "dp", 0, 0)


def across_dp(block):
    n = lax.axis_size("dp")

    def shifted(a, by):
        return lax.ppermute(a, "dp", [(i, (i + 2 * by) % n) for i in range(n)])

    other = lax.ppermute(block, "dp", [(i, i ^ 1) for i in range(n)])
    both = jnp.stack([block, other])
    length = n // 2
    held = [both] + [None] * (length - 1)
    for step in range(1, length // 2 + 1):
        held[step] = shifted(held[step - 1], 1)
        if step < length - step:
            held[length - step] = shifted(held[(length - step + 1) % length], -1)
    return jnp.concatenate(held, axis=0)


def tables(segs, head_size):
    batch, length = segs.shape
    index = jnp.arange(length, dtype=jnp.int32)
    earlier = jnp.sum((segs[:, None, :] < segs[:, :, None]).astype(jnp.int32), axis=-1)
    where_at = (index[None, :] - earlier).astype(F32).reshape(batch * length)
    half = head_size // 2
    freq = ROTARY_BASE ** (-2.0 * jnp.arange(half, dtype=F32) / head_size)
    angle = where_at[:, None] * freq
    cosine, sine = jnp.cos(angle), jnp.sin(angle)
    flat = segs.reshape(batch * length)
    token = jnp.arange(batch * length, dtype=jnp.int32)
    allowed = (
        (flat[:, None] == flat[None, :])
        & (token[:, None] >= token[None, :])
        & (token[:, None] // length == token[None, :] // length)
    )
    return (
        jnp.concatenate([cosine, cosine], axis=-1),
        jnp.concatenate([-sine, sine], axis=-1),
        allowed.astype(F32),
    )


def three(a):
    high = a.astype(BF16)
    rest = a - high.astype(F32)
    middle = rest.astype(BF16)
    return [high, middle, (rest - middle.astype(F32)).astype(BF16)]


def local(x_in, segment_ids, norm_gain, w_attn, final_gain, upstream):
    n = lax.axis_size("section")
    me = lax.axis_index("section")
    row = lax.axis_index("dp")
    micro_count, tok_count, width = x_in.shape
    rows = micro_count * tok_count
    part = width // n
    gain = norm_gain[0].astype(F32)
    last_gain = final_gain.astype(F32)
    weights = w_attn[0]
    hd = weights.shape[1] // 4
    w_in, w_out = weights[:, : 3 * hd], weights[:, 3 * hd :]
    x = x_in.reshape(rows, width)
    up = upstream.reshape(rows, width)

    def cut(a, index, axis=0):
        return lax.dynamic_slice_in_dim(a, index * part, part, axis)

    x32 = x.astype(F32)
    up_gain = up.astype(F32) * last_gain
    first = mm((x32 * gain).astype(BF16), w_in)
    second = mm(jnp.concatenate([x, up_gain.astype(BF16)], axis=0), w_out)
    high, low = split(first[:, : 2 * hd])
    square = jnp.sum(x32 * x32, axis=1, keepdims=True)
    reach = jnp.sum(x32 * up_gain, axis=1, keepdims=True)
    segs = segment_ids.reshape(rows, 1).astype(BF16)
    extra = jnp.concatenate(
        three(square) + three(reach) + [segs, jnp.zeros((rows, hd - 7), BF16)], axis=1
    )
    packed = jnp.concatenate(
        [high, low, first[:, 2 * hd :].astype(BF16), second[:rows].astype(BF16),
         second[rows:].astype(BF16), extra],
        axis=1,
    )
    packed = dp_move(packed)

    pairs = n // 2
    quarter = pairs // 2

    def slot(i):
        return (i % 2) * pairs + i // 2

    def turn(i, x_step, y_step):
        place = i // 2
        across = (place // quarter + x_step) % 2
        along_y = (place % quarter + y_step) % quarter
        return (across * quarter + along_y) * 2 + i % 2

    mine = swapped(cut(weights, slot(row))[:, 3 * hd :])
    near = jnp.concatenate([mine, along(mine, lambda i: turn(i, 1, 0))], axis=0)
    pieces = [near] + [
        along(near, lambda i, k=k: turn(i, 0, k)) for k in range(1, quarter)
    ]
    *pieces, packed = lax.optimization_barrier((*pieces, packed))
    pieces = pieces + [along(p, lambda i: i ^ 1) for p in pieces]
    order = []
    for core in range(2):
        for k in range(quarter):
            for x_step in range(2):
                order.append(slot(turn(me, x_step, -k) ^ core))
    order = jnp.stack(order).astype(jnp.int32)

    w_scaled = (cut(weights, row)[:, : 3 * hd].astype(F32) * cut(gain, row)[:, None]).astype(BF16)
    w_out_all = lax.all_gather(cut(weights, row)[:, 3 * hd :], "section")
    tokens = jnp.concatenate(
        [cut(x, me ^ row, 1).T,
         (cut(up, me ^ row, 1).astype(F32) * cut(last_gain, me ^ row)).astype(BF16).T],
        axis=1,
    )

    gains = gain.reshape(n, part)
    begun = couple(
        order[:pairs], weights, gains, jnp.zeros((hd, 4 * hd), F32), pieces[:quarter], F32
    )
    w_scaled, _, _ = lax.optimization_barrier((w_scaled, w_out_all, begun))
    w_in_all = lax.all_gather(w_scaled, "section")
    block = couple(order[pairs:], weights, gains, begun, pieces[quarter:], BF16)
    returned = swapped(block[:, 2 * hd :])
    on_diag = jnp.concatenate([block[:, 3 * hd :], jnp.zeros((hd, hd), BF16)], axis=1)
    shard = jnp.where(row < me, block[:, : 2 * hd], jnp.where(row == me, on_diag, returned))
    shards = all_of_dp(shard)
    ready, _ = lax.optimization_barrier((shards, w_in_all))
    blocks = lax.all_gather(ready, "section")
    packed, tokens, _ = lax.optimization_barrier((packed, tokens, shards))
    packed = section_move(packed)
    tokens = section_move(dp_move(tokens))
    base = across_dp(packed[:, : 7 * hd])
    tokens, base, blocks = lax.optimization_barrier((tokens, base, blocks))
    extra = packed[:, 7 * hd :].astype(F32)
    stats = jnp.concatenate([rowsum(extra[:, :3]), rowsum(extra[:, 3:6])], axis=1)
    cosine, sine, allowed = tables(
        extra[:, 6].astype(jnp.int32).reshape(micro_count, tok_count), hd
    )

    pick = jnp.stack([me, row]).astype(jnp.int32)
    zo, factors = scan_layers(pick, blocks, base, stats, cosine, sine, allowed, width)

    mine, theirs = all_terms(pick, w_in_all, w_out_all, zo, tokens, factors)
    theirs = along(theirs, lambda i: i ^ 1)
    mine = (mine.astype(F32) + theirs.astype(F32)).astype(BF16)
    total = lax.psum_scatter(
        mine,
        "section",
        scatter_dimension=0,
        axis_index_groups=[list(range(core, n, 2)) for core in range(2)],
        tiled=True,
    )
    factor = jnp.concatenate(
        [jnp.broadcast_to(cut(gain, row)[:, None], (part, 3 * hd)), jnp.ones((part, hd), F32)], axis=1
    )
    return (total.astype(F32) * factor).astype(BF16)


def solution(mesh):
    placed = (
        P("dp", None, None),
        P("dp", None),
        P("section", None),
        P("section", None, None),
        P(),
        P("dp", None, None),
    )
    return jax.shard_map(
        local, mesh=mesh, in_specs=placed, out_specs=P("section", "dp", None), check_vma=False
    )
```

```python
import functools

import jax
import jax.numpy as jnp
from jax import lax
from jax.experimental import pallas as pl
from jax.experimental.pallas import tpu as pltpu
from jax.sharding import PartitionSpec as P

EPSILON = 1e-05
ROTARY_BASE = 500000.0
F32 = jnp.float32
BF16 = jnp.bfloat16
NN = (((1,), (0,)), ((), ()))
NT = (((1,), (1,)), ((), ()))
TN = (((0,), (0,)), ((), ()))


def mm(a, b, dims=NN):
    return lax.dot_general(a, b, dims, preferred_element_type=F32)


def split(a):
    high = a.astype(BF16)
    return high, (a - high.astype(F32)).astype(BF16)


def mm3(a, b, dims=NN):
    (ah, al), (bh, bl) = a, b
    ((i,), (j,)), _ = dims
    both = mm(jnp.concatenate([ah, al], axis=i), jnp.concatenate([bh, bh], axis=j), dims)
    return both + mm(ah, bl, dims)


def rowsum(a):
    return jnp.sum(a, axis=1, keepdims=True)


def scan_kernel(
    layers, width, hd,
    pick, blocks, base, stats, cosine, sine, allowed,
    zo, factors,
    cols, diag, outs, grads, q_keep, k_keep, v_keep, p_keep, r_keep, s_keep, col_sem, diag_sem,
):
    first = [l * (l - 1) // 2 for l in range(layers + 1)]

    def copies(l):
        span = pl.ds(first[l], l)
        return (
            pltpu.make_async_copy(
                blocks.at[l, pl.ds(0, l)], cols.at[span, :, pl.ds(0, 2 * hd)], col_sem.at[0, l]
            ),
            pltpu.make_async_copy(
                blocks.at[pl.ds(0, l), l], cols.at[span, :, pl.ds(2 * hd, 2 * hd)], col_sem.at[1, l]
            ),
        )

    def diag_copy(l):
        return pltpu.make_async_copy(blocks.at[l, l, :, pl.ds(0, hd)], diag.at[l], diag_sem.at[l])

    for l in range(layers):
        diag_copy(l).start()
    for l in range(1, layers):
        for c in copies(l):
            c.start()

    def place(l):
        c = pick[0] ^ l
        return ((pick[1] // 2 + layers // 2 - c // 2) % (layers // 2)) * 2 + ((c ^ pick[1]) & 1)

    cosine, sine = cosine[...], sine[...]
    shut = allowed[...] == 0.0

    def rope(u):
        return u * cosine + pltpu.roll(u, hd // 2, 1) * sine

    def rope_back(w):
        return w * cosine - pltpu.roll(w, hd // 2, 1) * sine

    def start_of(l):
        own = base[place(l)]
        return jnp.concatenate(
            [
                own[:, : 2 * hd].astype(F32) + own[:, 2 * hd : 4 * hd].astype(F32),
                own[:, 4 * hd : 6 * hd].astype(F32),
            ],
            axis=1,
        )

    scale = hd ** (-0.5)
    inv_width = 1.0 / width
    square = stats[:, 0:1]
    reach = stats[:, 1:2]
    o = None
    early = layers // 3
    partial = start_of(0)
    for l in range(layers):
        if l in (0, early):
            for i in range(1, early + 1) if l == 0 else range(early + 1, layers):
                for c in copies(i):
                    c.wait()
            for i in range(early) if l == 0 else range(early, layers):
                diag_copy(i).wait()
        acc = partial
        if l:
            acc = acc + mm(o, cols[first[l] + l - 1])
        s = lax.rsqrt(square * inv_width + EPSILON)
        q = rope(acc[:, :hd] * s)
        k = rope(acc[:, hd : 2 * hd] * s)
        v = acc[:, 2 * hd : 3 * hd] * s
        reached = acc[:, 3 * hd :]
        scores = mm3(split(q), split(k), NT) * scale
        if l + 1 < layers:
            partial = start_of(l + 1)
            if l:
                rows = cols[pl.ds(first[l + 1], l)].reshape(l * hd, 4 * hd)
                partial = partial + mm(outs[:, pl.ds(0, l * hd)], rows)
        scores = jnp.where(shut, -1e30, scores)
        e = jnp.exp(scores - jnp.max(scores, axis=1, keepdims=True))
        inverse = 1.0 / rowsum(e)
        o = (mm(e.astype(BF16), v.astype(BF16)) * inverse).astype(BF16)
        outs[:, pl.ds(l * hd, hd)] = o
        zo[l, :, pl.ds(3 * hd, hd)] = o
        o32 = o.astype(F32)
        turned = mm(o, diag[l])
        square = jnp.maximum(square + rowsum(o32 * (2.0 * reached + turned)), 0.0)
        reach = reach + rowsum(o32 * base[place(l)][:, 6 * hd :].astype(F32))
        q_keep[l] = q
        k_keep[l] = k
        v_keep[l] = v
        p_keep[l] = e * inverse
        r_keep[l] = reached + turned
        s_keep[l] = jnp.broadcast_to(s, (s.shape[0], hd))

    s_last = lax.rsqrt(square * inv_width + EPSILON)
    back = s_last * s_last * s_last * inv_width * reach
    factors[layers] = jnp.broadcast_to(back, (back.shape[0], hd)).T[:8]
    factors[layers + 1] = jnp.broadcast_to(s_last, (back.shape[0], hd)).T[:8]
    for l in range(layers):
        grads[:, pl.ds(l * hd, hd)] = s_last * base[place(l)][:, 6 * hd :].astype(F32)

    waiting = None
    for l in range(layers - 1, -1, -1):
        d_o = grads[:, pl.ds(l * hd, hd)] - back * r_keep[l]
        if waiting is not None:
            d_o = d_o + mm(waiting, cols[first[l + 1] + l], NT)
        p, q, k, v, s = p_keep[l], q_keep[l], k_keep[l], v_keep[l], s_keep[l]
        d_o16 = d_o.astype(BF16)
        d_p = mm(d_o16, v.astype(BF16), NT)
        d_v = mm(p.astype(BF16), d_o16, TN)
        if waiting is not None and l:
            rows = cols[pl.ds(first[l + 1], l)].reshape(l * hd, 4 * hd)
            grads[:, pl.ds(0, l * hd)] += mm(waiting, rows, NT)
        d_s = p * (d_p - rowsum(d_p * p)) * scale
        ds = split(d_s)
        d_q = mm3(ds, split(k))
        d_k = mm3(ds, split(q), TN)
        c = rowsum(d_q * q + d_k * k + d_v * v) * (s[:, 0:1] * s[:, 0:1]) * inv_width
        o32 = outs[:, pl.ds(l * hd, hd)].astype(F32)
        z = jnp.concatenate(
            [rope_back(d_q) * s, rope_back(d_k) * s, d_v * s, -(back * o32)], axis=1
        ).astype(BF16)
        zo[l, :, pl.ds(0, 3 * hd)] = z[:, : 3 * hd]
        factors[l] = jnp.broadcast_to(c, (c.shape[0], hd)).T[:8]
        waiting = z
        back = back + c


def scan_layers(pick, blocks, base, stats, cosine, sine, allowed, width):
    layers, _, hd, _ = blocks.shape
    rows = base.shape[1]
    vmem = pl.BlockSpec(memory_space=pltpu.VMEM)
    keep = pltpu.VMEM((layers, rows, hd), F32)
    return pl.pallas_call(
        functools.partial(scan_kernel, layers, width, hd),
        out_shape=(
            jax.ShapeDtypeStruct((layers, rows, 4 * hd), BF16),
            jax.ShapeDtypeStruct((layers + 2, 8, rows), F32),
        ),
        in_specs=[pl.BlockSpec(memory_space=pltpu.SMEM), pl.BlockSpec(memory_space=pl.ANY)] + [vmem] * 5,
        out_specs=(vmem, vmem),
        scratch_shapes=[
            pltpu.VMEM((layers * (layers - 1) // 2, hd, 4 * hd), BF16),
            pltpu.VMEM((layers, hd, hd), BF16),
            pltpu.VMEM((rows, layers * hd), BF16),
            pltpu.VMEM((rows, layers * hd), F32),
            keep, keep, keep, keep, keep, keep,
            pltpu.SemaphoreType.DMA((2, layers)),
            pltpu.SemaphoreType.DMA((layers,)),
        ],
        compiler_params=pltpu.CompilerParams(vmem_limit_bytes=40 * 1024 * 1024),
        cost_estimate=pl.CostEstimate(
            flops=2 * 3 * layers * layers * rows * hd * 4 * hd,
            bytes_accessed=2 * layers * layers * hd * 2 * hd + 4 * layers * rows * 8 * hd,
            transcendentals=layers * rows * rows,
        ),
        name="scan_layers",
    )(pick, blocks, base, stats, cosine, sine, allowed)


def block_kernel(hd, part, order, weights, gain, *refs):
    pieces, out, w, sem = refs[:-3], refs[-3], refs[-2], refs[-1]
    count = w.shape[0]

    def copy(at):
        rows = pl.ds(pl.multiple_of(order[at] * part, part), part)
        return pltpu.make_async_copy(weights.at[rows], w.at[at], sem.at[at])

    for at in range(count):
        copy(at).start()
    first = jnp.zeros((hd, 3 * hd), F32)
    second = jnp.zeros((hd, hd), F32)
    at = 0
    for piece in pieces:
        for i in range(piece.shape[0] // part):
            turned = piece[pl.ds(i * part, part), :].astype(F32).T
            scaled = (turned * gain[pl.ds(order[at], 1), :]).astype(BF16)
            copy(at).wait()
            first = first + mm(scaled, w[at][:, : 3 * hd])
            second = second + mm(turned.astype(BF16), w[at][:, 3 * hd :])
            at += 1
    out[...] = jnp.concatenate([first, second], axis=1).astype(BF16)


def couple(order, weights, gain, pieces):
    hd = weights.shape[1] // 4
    count, part = gain.shape
    vmem = pl.BlockSpec(memory_space=pltpu.VMEM)
    return pl.pallas_call(
        functools.partial(block_kernel, hd, part),
        out_shape=jax.ShapeDtypeStruct((hd, 4 * hd), BF16),
        in_specs=[pl.BlockSpec(memory_space=pltpu.SMEM), pl.BlockSpec(memory_space=pl.ANY)]
        + [vmem] * (1 + len(pieces)),
        out_specs=vmem,
        scratch_shapes=[
            pltpu.VMEM((count, part, 4 * hd), BF16),
            pltpu.SemaphoreType.DMA((count,)),
        ],
        compiler_params=pltpu.CompilerParams(vmem_limit_bytes=48 * 1024 * 1024),
        cost_estimate=pl.CostEstimate(
            flops=2 * weights.size * hd, bytes_accessed=weights.size * 2, transcendentals=0
        ),
        name="couple",
    )(order, weights, gain, *pieces)


def put_terms(hd, first, zo, hs, gs, out):
    for i in range(out.shape[0]):
        l = 2 * i + first
        z = zo[l]
        out[i, :, pl.ds(0, 3 * hd)] = mm(hs[l], z[:, : 3 * hd]).astype(BF16)
        out[i, :, pl.ds(3 * hd, hd)] = mm(gs[l], z[:, 3 * hd :]).astype(BF16)


def hidden_kernel(layers, hd, w_out, zo, tokens, hs):
    rows = zo.shape[1]
    h = tokens[:, :rows].astype(F32)
    for l in range(layers):
        hs[l] = h.astype(BF16)
        h = h + mm(w_out[l], zo[l][:, 3 * hd :], NT)
    hs[layers] = h.astype(BF16)


def grad_kernel(layers, hd, w_in, zo, tokens, factors, hs, gs):
    rows = zo.shape[1]
    g = (
        tokens[:, rows:].astype(F32) * factors[layers + 1][:1]
        - hs[layers].astype(F32) * factors[layers][:1]
    )
    for l in range(layers - 1, -1, -1):
        gs[l] = g.astype(BF16)
        if l:
            z = zo[l]
            g = g + (mm(w_in[l], z[:, : 3 * hd], NT) - hs[l].astype(F32) * factors[l][:1])


def term_kernel(hd, first, zo, hs, gs, out):
    put_terms(hd, first[0], zo, hs, gs, out)


def all_terms(pick, w_in, w_out, zo, tokens, factors):
    layers, part, hd = w_out.shape
    rows = zo.shape[1]
    smem = pl.BlockSpec(memory_space=pltpu.SMEM)
    vmem = pl.BlockSpec(memory_space=pltpu.VMEM)
    params = pltpu.CompilerParams(vmem_limit_bytes=32 * 1024 * 1024)
    cost = pl.CostEstimate(
        flops=layers * part * rows * 8 * hd, bytes_accessed=8 * w_out.size, transcendentals=0
    )
    kind = jax.ShapeDtypeStruct((layers // 2, part, 4 * hd), BF16)
    hs = pl.pallas_call(
        functools.partial(hidden_kernel, layers, hd),
        out_shape=jax.ShapeDtypeStruct((layers + 1, part, rows), BF16),
        in_specs=[vmem] * 3,
        out_specs=vmem,
        compiler_params=params,
        cost_estimate=cost,
        name="hidden_states",
    )(w_out, zo, tokens)
    gs = pl.pallas_call(
        functools.partial(grad_kernel, layers, hd),
        out_shape=jax.ShapeDtypeStruct((layers, part, rows), BF16),
        in_specs=[vmem] * 5,
        out_specs=vmem,
        compiler_params=params,
        cost_estimate=cost,
        name="state_grads",
    )(w_in, zo, tokens, factors, hs)
    terms = pl.pallas_call(
        functools.partial(term_kernel, hd),
        out_shape=kind,
        in_specs=[smem, vmem, vmem, vmem],
        out_specs=vmem,
        compiler_params=pltpu.CompilerParams(vmem_limit_bytes=32 * 1024 * 1024),
        cost_estimate=cost,
        name="terms",
    )
    core = pick[:1] % 2
    theirs = terms(1 - core, zo, hs, gs)
    return terms(core, zo, hs, gs), theirs


def moved(block, to):
    n = lax.axis_size("section")
    route = []
    for a in range(n):
        for b in range(n):
            c, d = to(a, b)
            route.append((a * n + b, c * n + d))
    return lax.ppermute(block, ("section", "dp"), route)


def section_move(block):
    return moved(block, lambda a, b: (a ^ b, b))


def dp_move(block):
    return moved(block, lambda a, b: (a, a ^ b))


def swapped(block):
    return moved(block, lambda a, b: (b, a))


def along(block, move):
    n = lax.axis_size("section")
    return lax.ppermute(block, "section", [(i, move(i)) for i in range(n)])


def all_of_dp(block):
    n = lax.axis_size("dp")
    return lax.all_to_all(jnp.broadcast_to(block[None], (n,) + block.shape), "dp", 0, 0)


def across_dp(block):
    n = lax.axis_size("dp")

    def shifted(a, by):
        return lax.ppermute(a, "dp", [(i, (i + 2 * by) % n) for i in range(n)])

    other = lax.ppermute(block, "dp", [(i, i ^ 1) for i in range(n)])
    both = jnp.stack([block, other])
    length = n // 2
    held = [both] + [None] * (length - 1)
    for step in range(1, length // 2 + 1):
        held[step] = shifted(held[step - 1], 1)
        if step < length - step:
            held[length - step] = shifted(held[(length - step + 1) % length], -1)
    return jnp.concatenate(held, axis=0)


def tables(segs, head_size):
    batch, length = segs.shape
    index = jnp.arange(length, dtype=jnp.int32)
    earlier = jnp.sum((segs[:, None, :] < segs[:, :, None]).astype(jnp.int32), axis=-1)
    where_at = (index[None, :] - earlier).astype(F32).reshape(batch * length)
    half = head_size // 2
    freq = ROTARY_BASE ** (-2.0 * jnp.arange(half, dtype=F32) / head_size)
    angle = where_at[:, None] * freq
    cosine, sine = jnp.cos(angle), jnp.sin(angle)
    flat = segs.reshape(batch * length)
    token = jnp.arange(batch * length, dtype=jnp.int32)
    allowed = (
        (flat[:, None] == flat[None, :])
        & (token[:, None] >= token[None, :])
        & (token[:, None] // length == token[None, :] // length)
    )
    return (
        jnp.concatenate([cosine, cosine], axis=-1),
        jnp.concatenate([-sine, sine], axis=-1),
        allowed.astype(F32),
    )


def three(a):
    high = a.astype(BF16)
    rest = a - high.astype(F32)
    middle = rest.astype(BF16)
    return [high, middle, (rest - middle.astype(F32)).astype(BF16)]


def local(x_in, segment_ids, norm_gain, w_attn, final_gain, upstream):
    n = lax.axis_size("section")
    me = lax.axis_index("section")
    row = lax.axis_index("dp")
    micro_count, tok_count, width = x_in.shape
    rows = micro_count * tok_count
    part = width // n
    gain = norm_gain[0].astype(F32)
    last_gain = final_gain.astype(F32)
    weights = w_attn[0]
    hd = weights.shape[1] // 4
    w_in, w_out = weights[:, : 3 * hd], weights[:, 3 * hd :]
    x = x_in.reshape(rows, width)
    up = upstream.reshape(rows, width)

    def cut(a, index, axis=0):
        return lax.dynamic_slice_in_dim(a, index * part, part, axis)

    x32 = x.astype(F32)
    up_gain = up.astype(F32) * last_gain
    first = mm((x32 * gain).astype(BF16), w_in)
    second = mm(jnp.concatenate([x, up_gain.astype(BF16)], axis=0), w_out)
    high, low = split(first[:, : 2 * hd])
    square = jnp.sum(x32 * x32, axis=1, keepdims=True)
    reach = jnp.sum(x32 * up_gain, axis=1, keepdims=True)
    segs = segment_ids.reshape(rows, 1).astype(BF16)
    extra = jnp.concatenate(
        three(square) + three(reach) + [segs, jnp.zeros((rows, hd - 7), BF16)], axis=1
    )
    packed = jnp.concatenate(
        [high, low, first[:, 2 * hd :].astype(BF16), second[:rows].astype(BF16),
         second[rows:].astype(BF16), extra],
        axis=1,
    )
    packed = dp_move(packed)

    pairs = n // 2
    quarter = pairs // 2

    def slot(i):
        return (i % 2) * pairs + i // 2

    def turn(i, x_step, y_step):
        place = i // 2
        across = (place // quarter + x_step) % 2
        along_y = (place % quarter + y_step) % quarter
        return (across * quarter + along_y) * 2 + i % 2

    mine = swapped(cut(weights, slot(row))[:, 3 * hd :])
    near = jnp.concatenate([mine, along(mine, lambda i: turn(i, 1, 0))], axis=0)
    pieces = [near] + [
        along(near, lambda i, k=k: turn(i, 0, k)) for k in range(1, quarter)
    ]
    *pieces, packed = lax.optimization_barrier((*pieces, packed))
    pieces = pieces + [along(p, lambda i: i ^ 1) for p in pieces]
    order = []
    for core in range(2):
        for k in range(quarter):
            for x_step in range(2):
                order.append(slot(turn(me, x_step, -k) ^ core))
    order = jnp.stack(order).astype(jnp.int32)

    w_scaled = (cut(weights, row)[:, : 3 * hd].astype(F32) * cut(gain, row)[:, None]).astype(BF16)
    w_out_all = lax.all_gather(cut(weights, row)[:, 3 * hd :], "section")
    w_scaled, _, _ = lax.optimization_barrier((w_scaled, w_out_all, pieces[-1]))
    w_in_all = lax.all_gather(w_scaled, "section")
    tokens = jnp.concatenate(
        [cut(x, me ^ row, 1).T,
         (cut(up, me ^ row, 1).astype(F32) * cut(last_gain, me ^ row)).astype(BF16).T],
        axis=1,
    )

    block = couple(order, weights, gain.reshape(n, part), pieces)
    returned = swapped(block[:, 2 * hd :])
    on_diag = jnp.concatenate([block[:, 3 * hd :], jnp.zeros((hd, hd), BF16)], axis=1)
    shard = jnp.where(row < me, block[:, : 2 * hd], jnp.where(row == me, on_diag, returned))
    shards = all_of_dp(shard)
    ready, _ = lax.optimization_barrier((shards, w_in_all))
    blocks = lax.all_gather(ready, "section")
    packed, tokens, _ = lax.optimization_barrier((packed, tokens, shards))
    packed = section_move(packed)
    tokens = section_move(dp_move(tokens))
    base = across_dp(packed[:, : 7 * hd])
    tokens, base, blocks = lax.optimization_barrier((tokens, base, blocks))
    extra = packed[:, 7 * hd :].astype(F32)
    stats = jnp.concatenate([rowsum(extra[:, :3]), rowsum(extra[:, 3:6])], axis=1)
    cosine, sine, allowed = tables(
        extra[:, 6].astype(jnp.int32).reshape(micro_count, tok_count), hd
    )

    pick = jnp.stack([me, row]).astype(jnp.int32)
    zo, factors = scan_layers(pick, blocks, base, stats, cosine, sine, allowed, width)

    mine, theirs = all_terms(pick, w_in_all, w_out_all, zo, tokens, factors)
    theirs = along(theirs, lambda i: i ^ 1)
    mine = (mine.astype(F32) + theirs.astype(F32)).astype(BF16)
    total = lax.psum_scatter(
        mine,
        "section",
        scatter_dimension=0,
        axis_index_groups=[list(range(core, n, 2)) for core in range(2)],
        tiled=True,
    )
    factor = jnp.concatenate(
        [jnp.broadcast_to(cut(gain, row)[:, None], (part, 3 * hd)), jnp.ones((part, hd), F32)], axis=1
    )
    return (total.astype(F32) * factor).astype(BF16)


def solution(mesh):
    placed = (
        P("dp", None, None),
        P("dp", None),
        P("section", None),
        P("section", None, None),
        P(),
        P("dp", None, None),
    )
    return jax.shard_map(
        local, mesh=mesh, in_specs=placed, out_specs=P("section", "dp", None), check_vma=False
    )
```
